512 devices in a mesh: ens: 8 (over x, y_hi), dom: 64 (over z, y_lo, core).
Axes of the slice: x: 4, y: 8 (y_hi: 2, y_lo: 4; y = y_hi * 4 + y_lo), z: 8, core: 2. Of those that a mesh axis runs over, the one named last changes fastest.
Arguments:
- features: bfloat16 [8, 256, 128, 256], P('ens', None, 'dom'), may hold values from -6 to 6
- w_first: bfloat16 [256, 2304], replicated, may hold values from -0.125 to 0.125
- later_kernel_matrix: bfloat16 [100, 2304], replicated, may hold values from -0.125 to 0.125
- observed_state: float32 [100, 128, 256], P(None, 'dom'), may hold values from -6 to 6
- land: int32 [128, 256], P('dom'), may hold values 0 or 1
Outputs:
- ensemble_outlook: float32 [8, 100, 128, 256], P('ens', None, 'dom')
- grad_first: bfloat16 [256, 2304], replicated
- grad_second: bfloat16 [100, 2304], replicated
- loss: float32 [], replicated
The draws below stay inside these ranges and needn't reach their ends.
All inputs are finite; a program needn't handle non-finite values. No bound on the sum of `land` on one device may be relied on, other than what follows from the above.
Results may differ from the reference program's by a relative error of at most 0.008.
Values may be sent and summed in bfloat16 or wider, within the bound.
No kernel may reach another device: no remote copies, remote signals or barrier semaphores. Data moves between devices by JAX's collectives and lax.ppermute only.
A program may use at most 64 MiB of HBM per device.

```python
import jax
import jax.numpy as jnp
from jax import lax

C = 256
V = 100
LON = 256
MEMBERS = 8
LAT = 128


def touch_ends(values, stream_key, smallest, top_value):
    longest = values.shape.index(max(values.shape))
    spots = []
    for shift in (0, 1):
        where = [jax.random.randint(jax.random.fold_in(stream_key, axis), (), 0, length) for axis, length in enumerate(values.shape)]
        where[longest] = (where[longest] + shift) % values.shape[longest]
        spots.append(tuple(where))
    return values.at[spots[0]].set(smallest).at[spots[1]].set(top_value)


def levels(stream_key, extent, cuts, least, high):
    loudness = 1.0
    for dim, blocks in cuts:
        draws = jax.random.uniform(jax.random.fold_in(jax.random.fold_in(stream_key, 6), dim), (blocks,), jnp.float32, least / len(cuts), high / len(cuts))
        loudness = loudness * jnp.repeat(jnp.exp(draws), extent[dim] // blocks).reshape((-1,) + (1,) * (len(extent) - 1 - dim))
    return loudness


def scatter_about(key, shape, scale, reach, split=(), dtype=jnp.bfloat16):
    values = jax.random.normal(key, shape, jnp.float32) * scale
    if len(split) > 0:
        values = levels(key, shape, split, -0.22, 0.18) * values
    return jnp.clip(values, min=-reach, max=reach).astype(dtype)


def setup_inputs(seed: int = 0) -> dict:
    splits = jax.random.split(jax.random.key(seed), 6)
    return {
        "features": scatter_about(splits[0], (MEMBERS, C, LAT, LON), 1.0, 6.0, ((0, 8), (2, 64))),
        "w_first": scatter_about(splits[1], (C, 9 * C), (9 * C) ** -0.5, 0.125),
        "later_kernel_matrix": scatter_about(splits[2], (V, 9 * C), (9 * C) ** -0.5, 0.125),
        "observed_state": scatter_about(splits[3], (V, LAT, LON), 1.0, 6.0, ((1, 64),), jnp.float32),
        "land": touch_ends((jax.random.randint(splits[4], (LAT, LON), 0, 10) < 3).astype(jnp.int32), jax.random.fold_in(splits[4], 1), 0, 1),
    }


SOFTNESS = 0.25
LAND_WEIGHT = 2.0
LOSS_SCALE = 65536.0

def activate(values):
    return jax.nn.gelu(values, approximate=True)

def columns(padded, row_count):
    pieces = []
    for row_off in range(3):
        stripe = padded[:, row_off:row_off + row_count, :]
        for lon_off in range(3):
            pieces.append(jnp.roll(stripe, 1 - lon_off, axis=2))
    stacked = jnp.concatenate(pieces, axis=0)
    return stacked.reshape(stacked.shape[0], row_count * padded.shape[2])

def back_columns(padded, row_count):
    pieces = []
    for row_off in range(3):
        stripe = padded[:, 2 - row_off:2 - row_off + row_count, :]
        for lon_off in range(3):
            pieces.append(jnp.roll(stripe, lon_off - 1, axis=2))
    stacked = jnp.concatenate(pieces, axis=0)
    return stacked.reshape(stacked.shape[0], row_count * padded.shape[2])

def soft_abs(diff):
    return jnp.sqrt(diff * diff + SOFTNESS * SOFTNESS)

def misfits_per_member(chosen, emitted_quantities, observed_state, area_factor, mesh_points):
    members = emitted_quantities.shape[0]
    skill = (chosen - observed_state[None]) / soft_abs(chosen - observed_state[None]) / members
    spread = jnp.zeros_like(chosen)
    for other in range(members):
        diff = chosen - emitted_quantities[other][None]
        spread = spread + diff / soft_abs(diff)
    return LOSS_SCALE / mesh_points * area_factor[None, None] * (skill - spread / (members * (members - 1)))

def probabilistic_skill_total(emitted_quantities, observed_state, area_factor):
    members = emitted_quantities.shape[0]
    skill = lax.optimization_barrier(jnp.sum(soft_abs(emitted_quantities - observed_state[None]), axis=0)) / members
    pairs = jnp.zeros_like(skill)
    for first in range(members):
        for second in range(first + 1, members):
            pairs = pairs + soft_abs(emitted_quantities[first] - emitted_quantities[second])
    return jnp.sum(area_factor[None] * (skill - pairs / (members * (members - 1))))

def reference(features, w_first, later_kernel_matrix, observed_state, land):
    members, channels, lat_total, lon_count = features.shape
    variables = observed_state.shape[0]
    area_factor = 1.0 + LAND_WEIGHT * land.astype(jnp.float32)
    mesh_points = float(variables * lat_total * lon_count)

    def forward(member_index):
        padded = jnp.pad(member_index, ((0, 0), (1, 1), (0, 0)))
        cols_first = columns(padded, lat_total)
        before = jnp.dot(w_first, cols_first, preferred_element_type=jnp.float32)
        hidden = activate(before).astype(jnp.bfloat16).reshape(channels, lat_total, lon_count)
        second_columns = columns(jnp.pad(hidden, ((0, 0), (1, 1), (0, 0))), lat_total)
        result = jnp.dot(later_kernel_matrix, second_columns, preferred_element_type=jnp.float32)
        return (before, cols_first, second_columns, result.reshape(variables, lat_total, lon_count))

    def prediction_alone(member_index):
        return forward(member_index)[3]
    member_predictions = lax.map(prediction_alone, features)
    misfits_every_member = misfits_per_member(member_predictions, member_predictions, observed_state, area_factor, mesh_points).astype(jnp.bfloat16)
    loss = probabilistic_skill_total(member_predictions, observed_state, area_factor) / mesh_points
    w_back = later_kernel_matrix.reshape(variables, 9, channels).transpose(2, 1, 0).reshape(channels, 9 * variables)
    dims = (((1,), (1,)), ((), ()))

    def accumulate(carry, inputs):
        member_index, member_misfits = inputs
        before, cols_first, second_columns, unused = forward(member_index)
        err_pad = jnp.pad(member_misfits, ((0, 0), (1, 1), (0, 0)))
        back = jnp.dot(w_back, back_columns(err_pad, lat_total), preferred_element_type=jnp.float32)
        unused_out, pull = jax.vjp(activate, before)
        pre_grad = pull(back)[0].astype(jnp.bfloat16)
        err_flat = member_misfits.reshape(variables, lat_total * lon_count)
        grad_two = lax.dot_general(err_flat, second_columns, dims, preferred_element_type=jnp.float32)
        grad_one = lax.dot_general(pre_grad, cols_first, dims, preferred_element_type=jnp.float32)
        return ((carry[0] + grad_one, carry[1] + grad_two), None)
    start = (jnp.zeros((channels, 9 * channels), jnp.float32), jnp.zeros((variables, 9 * channels), jnp.float32))
    running_sums, unused_stack = lax.scan(accumulate, start, (features, misfits_every_member))
    return (member_predictions, running_sums[0].astype(jnp.bfloat16), running_sums[1].astype(jnp.bfloat16), loss)
```

```python
import jax
import jax.numpy as jnp
from jax import lax
from jax.sharding import Mesh
from jax.sharding import PartitionSpec as P

SOFTNESS = 0.25
LAND_WEIGHT = 2.0
LOSS_SCALE = 65536.0

ENS = ("x", "yh")
DOM = ("z", "yl", "c")
PARTS = {"x": 4, "yh": 2, "z": 8, "yl": 4, "c": 2}
F32 = jnp.float32
BF16 = jnp.bfloat16


def activate(values):
    return jax.nn.gelu(values, approximate=True)


def columns(padded, row_count):
    pieces = []
    for row_off in range(3):
        stripe = padded[:, row_off : row_off + row_count, :]
        for lon_off in range(3):
            pieces.append(jnp.roll(stripe, 1 - lon_off, axis=2))
    stacked = jnp.concatenate(pieces, axis=0)
    return stacked.reshape(stacked.shape[0], row_count * padded.shape[2])


def back_columns(padded, row_count):
    pieces = []
    for row_off in range(3):
        stripe = padded[:, 2 - row_off : 2 - row_off + row_count, :]
        for lon_off in range(3):
            pieces.append(jnp.roll(stripe, lon_off - 1, axis=2))
    stacked = jnp.concatenate(pieces, axis=0)
    return stacked.reshape(stacked.shape[0], row_count * padded.shape[2])


def soft_abs(diff):
    return jnp.sqrt(diff * diff + SOFTNESS * SOFTNESS)


def with_neighbours(array, width):
    size = lax.axis_size(DOM)
    up = [(i, i + 1) for i in range(size - 1)]
    down = [(j, i) for i, j in up]
    before = lax.ppermute(array[:, array.shape[1] - width :], DOM, up)
    after = lax.ppermute(array[:, :width], DOM, down)
    return jnp.concatenate([before, array, after], axis=1)


def exchange(array, axes):
    return lax.all_to_all(array, axes, 0, 0, tiled=True)


def body(features, w_first, later_kernel_matrix, observed_state, land):
    local = features[0]
    channels, row_count, lon_count = local.shape
    cells = row_count * lon_count
    variables = observed_state.shape[0]
    members = lax.axis_size(ENS)
    dom_size = lax.axis_size(DOM)
    dom = lax.axis_index(DOM)
    mesh_points = float(variables * row_count * dom_size * lon_count)

    padded = with_neighbours(local, 2)
    wide = row_count + 2
    pre_wide = jnp.dot(w_first, columns(padded, wide), preferred_element_type=F32)
    pre_wide = pre_wide.reshape(channels, wide, lon_count)
    row = jnp.arange(wide)
    inside = ((row > 0) | (dom > 0)) & ((row < wide - 1) | (dom < dom_size - 1))
    hidden_pad = jnp.where(inside[None, :, None], activate(pre_wide), 0.0).astype(BF16)
    before = pre_wide[:, 1 : 1 + row_count].reshape(channels, cells)
    second_columns = columns(hidden_pad, row_count)
    outlook = jnp.dot(later_kernel_matrix, second_columns, preferred_element_type=F32)

    share = -(-variables // members)
    spare = share * members - variables
    area = (1.0 + LAND_WEIGHT * land.astype(F32)).reshape(1, cells)
    mine = lax.axis_index(ENS) * share
    obs = jnp.pad(observed_state.reshape(variables, cells), ((0, spare), (0, 0)))
    obs = lax.dynamic_slice_in_dim(obs, mine, share, axis=0)
    every = exchange(
        jnp.pad(outlook, ((0, spare), (0, 0))).reshape(members, share, cells), ENS
    )
    real = (mine + jnp.arange(share) < variables)[:, None]
    slopes = [None] * members
    crps = jnp.zeros((share, cells), F32)
    pairs = jnp.zeros((share, cells), F32)
    for p in range(members):
        d = every[p] - obs
        square = d * d + SOFTNESS * SOFTNESS
        inverse = lax.rsqrt(square)
        crps = crps + square * inverse
        slopes[p] = d * inverse / members
    spread = [jnp.zeros((share, cells), F32)] * members
    for p in range(members):
        for q in range(p + 1, members):
            d = every[p] - every[q]
            square = d * d + SOFTNESS * SOFTNESS
            inverse = lax.rsqrt(square)
            pairs = pairs + square * inverse
            s = d * inverse
            spread[p] = spread[p] + s
            spread[q] = spread[q] - s
    count = members * (members - 1)
    score = area * (crps / members - pairs / count)
    partial_loss = jnp.sum(jnp.where(real, score, 0.0)) / mesh_points
    errors = jnp.stack(
        [LOSS_SCALE / mesh_points * area * (slopes[p] - spread[p] / count) for p in range(members)]
    ).astype(BF16)
    errors = exchange(errors, ENS).reshape(share * members, cells)[:variables]

    err_pad = with_neighbours(errors.reshape(variables, row_count, lon_count), 1)
    w_back = (
        later_kernel_matrix.reshape(variables, 9, channels)
        .transpose(2, 1, 0)
        .reshape(channels, 9 * variables)
    )
    back = jnp.dot(w_back, back_columns(err_pad, row_count), preferred_element_type=F32)
    unused_out, pull = jax.vjp(activate, before)
    pre_grad = pull(back)[0].astype(BF16)
    dims = (((1,), (1,)), ((), ()))
    cols_first = columns(padded[:, 1 : 1 + wide], row_count)
    grad_two = lax.dot_general(errors, second_columns, dims, preferred_element_type=F32)
    grad_one = lax.dot_general(pre_grad, cols_first, dims, preferred_element_type=F32)

    total_rows = 384
    width = grad_one.shape[1]
    loss_row = jnp.pad(partial_loss.reshape(1, 1), ((0, 0), (0, width - 1)))
    filler = jnp.zeros((total_rows - channels - variables - 1, width), F32)
    grads = jnp.concatenate([grad_one, grad_two, loss_row, filler], axis=0).astype(BF16)
    xc, y = ("x", "c"), ("yh", "yl")
    part = exchange(grads.reshape(8, 48, width), xc)
    part = jnp.sum(part.astype(F32), axis=0).astype(BF16)
    part = exchange(part.reshape(8, 6, width), y)
    part = jnp.sum(part.astype(F32), axis=0).astype(BF16)
    part = exchange(jnp.broadcast_to(part[None], (8, 6, width)), "z")
    part = jnp.sum(part.astype(F32), axis=0).astype(BF16)
    part = exchange(jnp.broadcast_to(part[None], (8, 6, width)), y)
    part = part.reshape(48, width)
    totals = lax.all_gather(part, xc, axis=0, tiled=True)
    return (
        outlook.reshape(1, variables, row_count, lon_count),
        totals[:channels],
        totals[channels : channels + variables],
        totals[channels + variables, 0].astype(F32),
    )


def solution(mesh):
    split = Mesh(mesh.devices.reshape(tuple(PARTS.values())), tuple(PARTS))
    placed = (P(ENS, None, DOM, None), P(), P(), P(None, DOM, None), P(DOM, None))
    return jax.shard_map(
        body,
        mesh=split,
        in_specs=placed,
        out_specs=(P(ENS, None, DOM, None), P(), P(), P()),
        check_vma=False,
    )
```

```python
import jax
import jax.numpy as jnp
from jax import lax
from jax.experimental import pallas as pl
from jax.experimental.pallas import tpu as pltpu
from jax.sharding import Mesh
from jax.sharding import PartitionSpec as P

SOFTNESS = 0.25
LAND_WEIGHT = 2.0
LOSS_SCALE = 65536.0
GELU_A = 0.7978845608028654
GELU_B = 0.044715

ENS = ("x", "yh")
DOM = ("z", "yl", "c")
Y = ("yh", "yl")
PARTS = {"x": 4, "yh": 2, "z": 8, "yl": 4, "c": 2}
F32 = jnp.float32
BF16 = jnp.bfloat16

C = 256
V = 100
LON = 256
ROWS = 2
CELLS = ROWS * LON
MEMBERS = 8
SHARE = 16
VPAD = 112
TAPS = 9
LANES = 128
TILES = TAPS * C // LANES
SECOND = TILES * C
LOSS = SECOND + TILES * VPAD
FLAT = 7168
VMEM = pl.BlockSpec(memory_space=pltpu.VMEM)
SMEM = pl.BlockSpec(memory_space=pltpu.SMEM)
PARAMS = pltpu.CompilerParams(vmem_limit_bytes=40 * 1024 * 1024)
NT = (((1,), (1,)), ((), ()))


def turn(values, shift):
    return values if shift % LON == 0 else pltpu.roll(values, shift % LON, 1)


def dot(a, b):
    return jnp.dot(a, b, preferred_element_type=F32)


def split(total):
    high = total.astype(BF16)
    return high, (total - high.astype(F32)).astype(BF16)


def forward_kernel(ends, before, local, after, w1, w2, hidden, slope, outlook, stack):
    rows = [r[:, i * LON : (i + 1) * LON] for r in (before, local, after) for i in range(2)]
    wide = ROWS + 2
    for a in range(3):
        for i in range(wide):
            stack[a * C : (a + 1) * C, i * LON : (i + 1) * LON] = rows[i + a]
    for i in range(wide):
        lanes = slice(i * LON, (i + 1) * LON)
        pre = None
        for b in range(3):
            taps = jnp.concatenate(
                [w1[:, (3 * a + b) * C : (3 * a + b + 1) * C] for a in range(3)], axis=1
            )
            part = turn(dot(taps, stack[:, lanes]), 1 - b)
            pre = part if pre is None else pre + part
        square = pre * pre
        t = jnp.tanh(GELU_A * pre * (1.0 + GELU_B * square))
        half = 0.5 * (1.0 + t)
        value = pre * half
        if i == 0:
            value = value * ends[0]
        if i == wide - 1:
            value = value * ends[1]
        hidden[:, lanes] = value.astype(BF16)
        if 0 < i < wide - 1:
            own = slice((i - 1) * LON, i * LON)
            slope[:, own] = half + (0.5 * GELU_A) * pre * (1.0 - t * t) * (
                1.0 + 3.0 * GELU_B * square
            )
    outlook[V:, :] = jnp.zeros((MEMBERS * SHARE - V, CELLS), F32)
    for i in range(ROWS):
        total = None
        for b in range(3):
            part = None
            for a in range(3):
                tap = w2[:, (3 * a + b) * C : (3 * a + b + 1) * C]
                term = dot(tap, hidden[:, (i + a) * LON : (i + a + 1) * LON])
                part = term if part is None else part + term
            part = turn(part, 1 - b)
            total = part if total is None else total + part
        outlook[:V, i * LON : (i + 1) * LON] = total


def score_kernel(points, me, every, obs, land, errors, loss):
    area = 1.0 + LAND_WEIGHT * land[...].astype(F32)
    x = [every[p] for p in range(MEMBERS)]
    truth = obs[me[0]]
    count = MEMBERS * (MEMBERS - 1)
    skill = pairs = jnp.zeros((SHARE, CELLS), F32)
    slopes = []
    for p in range(MEMBERS):
        d = x[p] - truth
        square = d * d + SOFTNESS * SOFTNESS
        inverse = lax.rsqrt(square)
        skill = skill + square * inverse
        slopes.append(d * inverse * (1.0 / MEMBERS))
    for p in range(MEMBERS):
        for q in range(p + 1, MEMBERS):
            d = x[p] - x[q]
            square = d * d + SOFTNESS * SOFTNESS
            inverse = lax.rsqrt(square)
            pairs = pairs + square * inverse
            s = d * inverse * (1.0 / count)
            slopes[p] = slopes[p] - s
            slopes[q] = slopes[q] + s
    variable = me[0] * SHARE + lax.broadcasted_iota(jnp.int32, (SHARE, CELLS), 0)
    crps = area * (skill * (1.0 / MEMBERS) - pairs * (1.0 / count))
    crps = jnp.where(variable < V, crps, 0.0)
    loss[...] = jnp.sum(crps, axis=(0, 1), keepdims=True) * (1.0 / points)
    factor = area * (LOSS_SCALE / points)
    for p in range(MEMBERS):
        errors[p] = (factor * slopes[p]).astype(BF16)


def backward_kernel(
    loss, err, err_before, err_after, w_back, slope, hidden, before, local, after, out, e, pg
):
    rows = [err_before[...], err[:VPAD, :LON], err[:VPAD, LON:], err_after[...]]
    for i in range(4):
        row = rows[i].astype(F32)
        for b in range(3):
            e[b * VPAD : (b + 1) * VPAD, i * LON : (i + 1) * LON] = turn(row, b - 1).astype(BF16)
    for i in range(ROWS):
        back = None
        for a in range(3):
            start = (i + 2 - a) * LON
            term = dot(w_back[a], e[:, start : start + LON])
            back = term if back is None else back + term
        own = slice(i * LON, (i + 1) * LON)
        grad = back * slope[:, own]
        for b in range(3):
            pg[b * C : (b + 1) * C, own] = turn(grad, b - 1).astype(BF16)
    for a in range(3):
        if a == 0:
            window = jnp.concatenate([before[:, LON:], local[:, :LON]], axis=1)
        elif a == 1:
            window = local[...]
        else:
            window = jnp.concatenate([local[:, LON:], after[:, :LON]], axis=1)
        for b in range(3):
            first = lax.dot_general(
                pg[b * C : (b + 1) * C, :], window, NT, preferred_element_type=F32
            ).astype(BF16)
            second = lax.dot_general(
                e[b * VPAD : (b + 1) * VPAD, LON : 3 * LON],
                hidden[:, a * LON : a * LON + CELLS],
                NT,
                preferred_element_type=F32,
            ).astype(BF16)
            for part in range(2):
                tile = 2 * (3 * a + b) + part
                lanes = slice(part * LANES, (part + 1) * LANES)
                out[tile * C : (tile + 1) * C, :] = first[:, lanes]
                at = SECOND + tile * VPAD
                out[at : at + VPAD, :] = second[:, lanes]
    high, low = split(jnp.broadcast_to(loss[...], (1, LANES)))
    out[LOSS:, :] = jnp.zeros((FLAT - LOSS, LANES), BF16)
    row = lax.broadcasted_iota(jnp.int32, (16, LANES), 0)
    both = jnp.where(row == 0, high.astype(F32), jnp.where(row == 1, low.astype(F32), 0.0))
    out[LOSS : LOSS + 16, :] = both.astype(BF16)


def sum_kernel(row, holder, parts, out):
    total = parts[0].astype(F32)
    for i in range(1, parts.shape[0]):
        total = total + parts[i].astype(F32)
    copies = out.shape[0]
    value = total.astype(BF16)
    for i in range(copies):
        out[i] = value

    @pl.when(holder[0] == 1)
    def _():
        here = total[row : row + 16]
        loss = here[0:1] + here[1:2]
        high, low = split(loss)
        index = lax.broadcasted_iota(jnp.int32, (16, LANES), 0)
        fixed = jnp.where(index == 0, high.astype(F32), jnp.where(index == 1, low.astype(F32), 0.0))
        for i in range(copies):
            out[i, row : row + 16, :] = fixed.astype(BF16)


def summed(parts, row, holder, copies=1):
    body = lambda *refs: sum_kernel(row, *refs)
    return pl.pallas_call(
        body,
        out_shape=jax.ShapeDtypeStruct((copies,) + parts.shape[1:], BF16),
        in_specs=[SMEM, VMEM],
        out_specs=VMEM,
        compiler_params=PARAMS,
    )(holder, parts)


def last_kernel(halves, first, second, loss):
    flat = lambda at, n: halves[at : at + n, :]
    for tile in range(TILES):
        lanes = slice(tile * LANES, (tile + 1) * LANES)
        first[:, lanes] = flat(tile * C, C)
        second[:, lanes] = flat(SECOND + tile * VPAD, VPAD)[:V]
    here = flat(LOSS, 16).astype(F32)
    loss[...] = here[0:1, 0:1] + here[1:2, 0:1]


def exchange(array, axes):
    return lax.all_to_all(array, axes, 0, 0, tiled=True)


def body(features, w_first, later_kernel_matrix, observed_state, land):
    dom_size = lax.axis_size(DOM)
    dom = lax.axis_index(DOM)
    up = [(i, i + 1) for i in range(dom_size - 1)]
    down = [(j, i) for i, j in up]
    points = float(V * ROWS * dom_size * LON)

    local = features.reshape(C, CELLS)
    before = lax.ppermute(local, DOM, up)
    after = lax.ppermute(local, DOM, down)
    ends = jnp.stack([(dom > 0).astype(F32), (dom < dom_size - 1).astype(F32)])
    hidden, slope, outlook = pl.pallas_call(
        forward_kernel,
        out_shape=(
            jax.ShapeDtypeStruct((C, 4 * LON), BF16),
            jax.ShapeDtypeStruct((C, CELLS), F32),
            jax.ShapeDtypeStruct((MEMBERS * SHARE, CELLS), F32),
        ),
        in_specs=[SMEM] + [VMEM] * 5,
        out_specs=(VMEM,) * 3,
        scratch_shapes=[pltpu.VMEM((3 * C, 4 * LON), BF16)],
        compiler_params=PARAMS,
    )(ends, before, local, after, w_first, later_kernel_matrix)

    every = exchange(outlook.reshape(MEMBERS, SHARE, CELLS), ENS)
    obs = jnp.pad(observed_state.reshape(V, CELLS), ((0, MEMBERS * SHARE - V), (0, 0)))
    me = lax.axis_index(ENS).reshape(1)
    errors, loss = pl.pallas_call(
        lambda *refs: score_kernel(points, *refs),
        out_shape=(
            jax.ShapeDtypeStruct((MEMBERS, SHARE, CELLS), BF16),
            jax.ShapeDtypeStruct((1, 1), F32),
        ),
        in_specs=[SMEM] + [VMEM] * 3,
        out_specs=(VMEM,) * 2,
        compiler_params=PARAMS,
    )(me, every, obs.reshape(MEMBERS, SHARE, CELLS), land.reshape(1, CELLS))
    errors = exchange(errors, ENS).reshape(MEMBERS * SHARE, CELLS)

    err_before = lax.ppermute(errors[:VPAD, LON:], DOM, up)
    err_after = lax.ppermute(errors[:VPAD, :LON], DOM, down)
    w_back = later_kernel_matrix.reshape(V, 3, 3, C)
    w_back = jnp.pad(w_back, ((0, VPAD - V), (0, 0), (0, 0), (0, 0)))
    w_back = w_back.transpose(1, 3, 2, 0).reshape(3, C, 3 * VPAD)
    flat = pl.pallas_call(
        backward_kernel,
        out_shape=jax.ShapeDtypeStruct((FLAT, LANES), BF16),
        in_specs=[VMEM] * 10,
        out_specs=VMEM,
        scratch_shapes=[
            pltpu.VMEM((3 * VPAD, 4 * LON), BF16),
            pltpu.VMEM((3 * C, CELLS), BF16),
        ],
        compiler_params=PARAMS,
    )(loss, errors, err_before, err_after, w_back, slope, hidden, before, local, after)

    holder = jnp.bool_(True)
    row = LOSS
    size = FLAT
    part = flat
    for axes, n in (("c", 2), ("x", 4), (Y, 8)):
        size //= n
        holder = holder & (lax.axis_index(axes) == row // size)
        row %= size
        part = exchange(part.reshape(n, size, LANES), axes)
        flag = holder.astype(jnp.int32).reshape(1)
        part = summed(part, row, flag, 8 if axes == Y else 1)
    part = summed(exchange(part, "z"), row, flag, 8)
    part = exchange(part, Y).reshape(1, 8 * size, LANES)
    part = exchange(jnp.broadcast_to(part, (4, 8 * size, LANES)), "x").reshape(1, 32 * size, LANES)
    part = exchange(jnp.broadcast_to(part, (2, 32 * size, LANES)), "c").reshape(FLAT, LANES)
    first, second, loss = pl.pallas_call(
        last_kernel,
        out_shape=(
            jax.ShapeDtypeStruct((C, TAPS * C), BF16),
            jax.ShapeDtypeStruct((V, TAPS * C), BF16),
            jax.ShapeDtypeStruct((1, 1), F32),
        ),
        in_specs=[VMEM],
        out_specs=(VMEM,) * 3,
        compiler_params=PARAMS,
    )(part)
    return outlook[:V].reshape(1, V, ROWS, LON), first, second, loss.reshape(())


def solution(mesh):
    split_mesh = Mesh(mesh.devices.reshape(tuple(PARTS.values())), tuple(PARTS))
    placed = (P(ENS, None, DOM, None), P(), P(), P(None, DOM, None), P(DOM, None))
    return jax.shard_map(
        body,
        mesh=split_mesh,
        in_specs=placed,
        out_specs=(P(ENS, None, DOM, None), P(), P(), P()),
        check_vma=False,
    )
```

```python
import jax
import jax.numpy as jnp
from jax import lax
from jax.experimental import pallas as pl
from jax.experimental.pallas import tpu as pltpu
from jax.sharding import Mesh
from jax.sharding import PartitionSpec as P

SOFTNESS = 0.25
LAND_WEIGHT = 2.0
LOSS_SCALE = 65536.0
GELU_A = 0.7978845608028654
GELU_B = 0.044715

ENS = ("x", "yh")
DOM = ("z", "yl", "c")
Y = ("yh", "yl")
PARTS = {"x": 4, "yh": 2, "z": 8, "yl": 4, "c": 2}
F32 = jnp.float32
BF16 = jnp.bfloat16

C = 256
V = 100
LON = 256
ROWS = 2
CELLS = ROWS * LON
MEMBERS = 8
SHARE = 16
VPAD = 112
TAPS = 9
LANES = 128
TILES = TAPS * C // LANES
SECOND = TILES * C
LOSS = SECOND + TILES * VPAD
FLAT = 6656
HALF = FLAT // 2
VMEM = pl.BlockSpec(memory_space=pltpu.VMEM)
SMEM = pl.BlockSpec(memory_space=pltpu.SMEM)
PARAMS = pltpu.CompilerParams(vmem_limit_bytes=40 * 1024 * 1024)
NT = (((1,), (1,)), ((), ()))


def turn(values, shift):
    return values if shift % LON == 0 else pltpu.roll(values, shift % LON, 1)


def dot(a, b):
    return jnp.dot(a, b, preferred_element_type=F32)


def split(total):
    high = total.astype(BF16)
    return high, (total - high.astype(F32)).astype(BF16)


def prepare_kernel(w1, w2, w1_out, w2_out, w_back):
    w1_out[...] = w1[...]
    w2_out[...] = w2[...]
    spare = jnp.zeros((C, VPAD - V), F32)
    for a in range(3):
        turned = []
        for b in range(3):
            tap = w2[:, (3 * a + b) * C : (3 * a + b + 1) * C].astype(F32)
            turned += [tap.T, spare]
        w_back[a] = jnp.concatenate(turned, axis=1).astype(BF16)


def forward_kernel(ends, before, local, after, w1, w2, hidden, slope, outlook, sent, stack):
    rows = [r[:, i * LON : (i + 1) * LON] for r in (before, local, after) for i in range(2)]
    wide = ROWS + 2
    for a in range(3):
        for i in range(wide):
            stack[a * C : (a + 1) * C, i * LON : (i + 1) * LON] = rows[i + a]
    for i in range(wide):
        lanes = slice(i * LON, (i + 1) * LON)
        pre = None
        for b in range(3):
            taps = jnp.concatenate(
                [w1[:, (3 * a + b) * C : (3 * a + b + 1) * C] for a in range(3)], axis=1
            )
            part = turn(dot(taps, stack[:, lanes]), 1 - b)
            pre = part if pre is None else pre + part
        square = pre * pre
        t = jnp.tanh(GELU_A * pre * (1.0 + GELU_B * square))
        half = 0.5 * (1.0 + t)
        value = pre * half
        if i == 0:
            value = value * ends[0]
        if i == wide - 1:
            value = value * ends[1]
        hidden[:, lanes] = value.astype(BF16)
        if 0 < i < wide - 1:
            own = slice((i - 1) * LON, i * LON)
            slope[:, own] = half + (0.5 * GELU_A) * pre * (1.0 - t * t) * (
                1.0 + 3.0 * GELU_B * square
            )
    top = V // 16 * 16
    sent[top:, :] = jnp.zeros((MEMBERS * SHARE - top, CELLS), BF16)
    spare = jnp.zeros((VPAD - V, LON), F32)
    for i in range(ROWS):
        total = None
        for b in range(3):
            part = None
            for a in range(3):
                tap = w2[:, (3 * a + b) * C : (3 * a + b + 1) * C]
                term = dot(tap, hidden[:, (i + a) * LON : (i + a + 1) * LON])
                part = term if part is None else part + term
            part = turn(part, 1 - b)
            total = part if total is None else total + part
        lanes = slice(i * LON, (i + 1) * LON)
        outlook[:, lanes] = total
        sent[:VPAD, lanes] = jnp.concatenate([total, spare], axis=0).astype(BF16)


def score_kernel(points, me, every, obs, land, errors, loss):
    area = 1.0 + LAND_WEIGHT * land[...].astype(F32)
    x = [every[p].astype(F32) for p in range(MEMBERS)]
    truth = obs[me[0]]
    count = MEMBERS * (MEMBERS - 1)
    skill = pairs = jnp.zeros((SHARE, CELLS), F32)
    slopes = []
    for p in range(MEMBERS):
        d = x[p] - truth
        square = d * d + SOFTNESS * SOFTNESS
        inverse = lax.rsqrt(square)
        skill = skill + square * inverse
        slopes.append(d * inverse * (1.0 / MEMBERS))
    for p in range(MEMBERS):
        for q in range(p + 1, MEMBERS):
            d = x[p] - x[q]
            square = d * d + SOFTNESS * SOFTNESS
            inverse = lax.rsqrt(square)
            pairs = pairs + square * inverse
            s = d * inverse * (1.0 / count)
            slopes[p] = slopes[p] - s
            slopes[q] = slopes[q] + s
    variable = me[0] * SHARE + lax.broadcasted_iota(jnp.int32, (SHARE, CELLS), 0)
    crps = area * (skill * (1.0 / MEMBERS) - pairs * (1.0 / count))
    crps = jnp.where(variable < V, crps, 0.0)
    loss[...] = jnp.sum(crps, axis=(0, 1), keepdims=True) * (1.0 / points)
    factor = area * (LOSS_SCALE / points)
    for p in range(MEMBERS):
        errors[p] = (factor * slopes[p]).astype(BF16)


def backward_kernel(
    loss, err, err_before, err_after, w_back, slope, hidden, before, local, after, out, e, pg
):
    rows = [err_before[...], err[:VPAD, :LON], err[:VPAD, LON:], err_after[...]]
    for i in range(4):
        row = rows[i].astype(F32)
        for b in range(3):
            e[b * VPAD : (b + 1) * VPAD, i * LON : (i + 1) * LON] = turn(row, b - 1).astype(BF16)
    for i in range(ROWS):
        back = None
        for a in range(3):
            start = (i + 2 - a) * LON
            term = dot(w_back[a], e[:, start : start + LON])
            back = term if back is None else back + term
        own = slice(i * LON, (i + 1) * LON)
        grad = back * slope[:, own]
        for b in range(3):
            pg[b * C : (b + 1) * C, own] = turn(grad, b - 1).astype(BF16)
    for a in range(3):
        if a == 0:
            window = jnp.concatenate([before[:, LON:], local[:, :LON]], axis=1)
        elif a == 1:
            window = local[...]
        else:
            window = jnp.concatenate([local[:, LON:], after[:, :LON]], axis=1)
        for b in range(3):
            first = lax.dot_general(
                pg[b * C : (b + 1) * C, :], window, NT, preferred_element_type=F32
            ).astype(BF16)
            second = lax.dot_general(
                e[b * VPAD : (b + 1) * VPAD, LON : 3 * LON],
                hidden[:, a * LON : a * LON + CELLS],
                NT,
                preferred_element_type=F32,
            ).astype(BF16)
            for part in range(2):
                tile = 2 * (3 * a + b) + part
                lanes = slice(part * LANES, (part + 1) * LANES)
                out[tile * C : (tile + 1) * C, :] = first[:, lanes]
                at = SECOND + tile * VPAD
                out[at : at + VPAD, :] = second[:, lanes]
    high, low = split(jnp.broadcast_to(loss[...], (1, LANES)))
    out[LOSS:, :] = jnp.zeros((FLAT - LOSS, LANES), BF16)
    row = lax.broadcasted_iota(jnp.int32, (16, LANES), 0)
    both = jnp.where(row == 0, high.astype(F32), jnp.where(row == 1, low.astype(F32), 0.0))
    out[LOSS : LOSS + 16, :] = both.astype(BF16)


def sum_kernel(row, holder, parts, out):
    total = parts[0].astype(F32)
    for i in range(1, parts.shape[0]):
        total = total + parts[i].astype(F32)
    copies = out.shape[0]
    value = total.astype(BF16)
    for i in range(copies):
        out[i] = value
    base = row // 16 * 16 if row + 16 <= total.shape[0] and row % 16 == 0 else 0
    span = 16 if row % 16 == 0 else total.shape[0]

    @pl.when(holder[0] == 1)
    def _():
        here = total[base : base + span]
        high, low = split(total[row : row + 1] + total[row + 1 : row + 2])
        index = lax.broadcasted_iota(jnp.int32, (span, LANES), 0) + base
        fixed = jnp.where(index == row, high.astype(F32), here)
        fixed = jnp.where(index == row + 1, low.astype(F32), fixed)
        for i in range(copies):
            out[i, base : base + span, :] = fixed.astype(BF16)


def summed(parts, row, holder, copies=1):
    body = lambda *refs: sum_kernel(row, *refs)
    return pl.pallas_call(
        body,
        out_shape=jax.ShapeDtypeStruct((copies,) + parts.shape[1:], BF16),
        in_specs=[SMEM, VMEM],
        out_specs=VMEM,
        compiler_params=PARAMS,
    )(holder, parts)


def last_kernel(core, own, other, first, second, loss):
    def assemble(low, high):
        def flat(at, n):
            return low[at : at + n, :] if at < HALF else high[at - HALF : at - HALF + n, :]

        for tile in range(TILES):
            lanes = slice(tile * LANES, (tile + 1) * LANES)
            first[:, lanes] = flat(tile * C, C)
            second[:, lanes] = flat(SECOND + tile * VPAD, VPAD)[:V]
        here = flat(LOSS, 16).astype(F32)
        loss[...] = here[0:1, 0:1] + here[1:2, 0:1]

    pl.when(core[0] == 0)(lambda: assemble(own, other))
    pl.when(core[0] == 1)(lambda: assemble(other, own))


def exchange(array, axes):
    return lax.all_to_all(array, axes, 0, 0, tiled=True)


def body(features, w_first, later_kernel_matrix, observed_state, land):
    dom_size = lax.axis_size(DOM)
    dom = lax.axis_index(DOM)
    up = [(i, i + 1) for i in range(dom_size - 1)]
    down = [(j, i) for i, j in up]
    points = float(V * ROWS * dom_size * LON)

    local = features.reshape(C, CELLS)
    before = lax.ppermute(local, DOM, up)
    after = lax.ppermute(local, DOM, down)
    w1, w2, w_back = pl.pallas_call(
        prepare_kernel,
        out_shape=(
            jax.ShapeDtypeStruct((C, TAPS * C), BF16),
            jax.ShapeDtypeStruct((V, TAPS * C), BF16),
            jax.ShapeDtypeStruct((3, C, 3 * VPAD), BF16),
        ),
        in_specs=[VMEM] * 2,
        out_specs=(VMEM,) * 3,
        compiler_params=PARAMS,
    )(w_first, later_kernel_matrix)
    ends = jnp.stack([(dom > 0).astype(F32), (dom < dom_size - 1).astype(F32)])
    hidden, slope, outlook, sent = pl.pallas_call(
        forward_kernel,
        out_shape=(
            jax.ShapeDtypeStruct((C, 4 * LON), BF16),
            jax.ShapeDtypeStruct((C, CELLS), F32),
            jax.ShapeDtypeStruct((V, CELLS), F32),
            jax.ShapeDtypeStruct((MEMBERS * SHARE, CELLS), BF16),
        ),
        in_specs=[SMEM] + [VMEM] * 5,
        out_specs=(VMEM,) * 4,
        scratch_shapes=[pltpu.VMEM((3 * C, 4 * LON), BF16)],
        compiler_params=PARAMS,
    )(ends, before, local, after, w1, w2)

    every = exchange(sent.reshape(MEMBERS, SHARE, CELLS), ENS)
    obs = jnp.pad(observed_state.reshape(V, CELLS), ((0, MEMBERS * SHARE - V), (0, 0)))
    me = lax.axis_index(ENS).reshape(1)
    errors, loss = pl.pallas_call(
        lambda *refs: score_kernel(points, *refs),
        out_shape=(
            jax.ShapeDtypeStruct((MEMBERS, SHARE, CELLS), BF16),
            jax.ShapeDtypeStruct((1, 1), F32),
        ),
        in_specs=[SMEM] + [VMEM] * 3,
        out_specs=(VMEM,) * 2,
        compiler_params=PARAMS,
    )(me, every, obs.reshape(MEMBERS, SHARE, CELLS), land.reshape(1, CELLS))
    errors = exchange(errors, ENS).reshape(MEMBERS * SHARE, CELLS)

    err_before = lax.ppermute(errors[:VPAD, LON:], DOM, up)
    err_after = lax.ppermute(errors[:VPAD, :LON], DOM, down)
    flat = pl.pallas_call(
        backward_kernel,
        out_shape=jax.ShapeDtypeStruct((FLAT, LANES), BF16),
        in_specs=[VMEM] * 10,
        out_specs=VMEM,
        scratch_shapes=[
            pltpu.VMEM((3 * VPAD, 4 * LON), BF16),
            pltpu.VMEM((3 * C, CELLS), BF16),
        ],
        compiler_params=PARAMS,
    )(loss, errors, err_before, err_after, w_back, slope, hidden, before, local, after)

    holder = jnp.bool_(True)
    row = LOSS
    size = FLAT
    part = flat
    for axes, n in (("c", 2), ("x", 4), (Y, 8)):
        size //= n
        holder = holder & (lax.axis_index(axes) == row // size)
        row %= size
        part = exchange(part.reshape(n, size, LANES), axes)
        flag = holder.astype(jnp.int32).reshape(1)
        part = summed(part, row, flag, 8 if axes == Y else 1)
    part = summed(exchange(part, "z"), row, flag, 8)
    part = exchange(part, Y).reshape(8 * size, LANES)
    part = lax.all_gather(part, "x", axis=0, tiled=True)
    other = lax.ppermute(part, "c", [(0, 1), (1, 0)])
    core = lax.axis_index("c").reshape(1)
    first, second, loss = pl.pallas_call(
        last_kernel,
        out_shape=(
            jax.ShapeDtypeStruct((C, TAPS * C), BF16),
            jax.ShapeDtypeStruct((V, TAPS * C), BF16),
            jax.ShapeDtypeStruct((1, 1), F32),
        ),
        in_specs=[SMEM, VMEM, VMEM],
        out_specs=(VMEM,) * 3,
        compiler_params=PARAMS,
    )(core, part, other)
    return outlook.reshape(1, V, ROWS, LON), first, second, loss.reshape(())


def solution(mesh):
    split_mesh = Mesh(mesh.devices.reshape(tuple(PARTS.values())), tuple(PARTS))
    placed = (P(ENS, None, DOM, None), P(), P(), P(None, DOM, None), P(DOM, None))
    return jax.shard_map(
        body,
        mesh=split_mesh,
        in_specs=placed,
        out_specs=(P(ENS, None, DOM, None), P(), P(), P()),
        check_vma=False,
    )
```

```python
import jax
import jax.numpy as jnp
from jax import lax
from jax.experimental import pallas as pl
from jax.experimental.pallas import tpu as pltpu
from jax.sharding import Mesh
from jax.sharding import PartitionSpec as P

SOFTNESS = 0.25
LAND_WEIGHT = 2.0
LOSS_SCALE = 65536.0
GELU_A = 0.7978845608028654
GELU_B = 0.044715

ENS = ("x", "yh")
DOM = ("z", "yl", "c")
Y = ("yh", "yl")
PARTS = {"x": 4, "yh": 2, "z": 8, "yl": 4, "c": 2}
F32 = jnp.float32
BF16 = jnp.bfloat16

C = 256
V = 100
LON = 256
ROWS = 2
CELLS = ROWS * LON
MEMBERS = 8
SHARE = 16
VPAD = 112
TAPS = 9
LANES = 128
TILES = TAPS * C // LANES
SECOND = TILES * C
LOSS = SECOND + TILES * VPAD
FLAT = 6656
HALF = FLAT // 2
VMEM = pl.BlockSpec(memory_space=pltpu.VMEM)
SMEM = pl.BlockSpec(memory_space=pltpu.SMEM)
PARAMS = pltpu.CompilerParams(vmem_limit_bytes=40 * 1024 * 1024)
NT = (((1,), (1,)), ((), ()))


def turn(values, shift):
    return values if shift % LON == 0 else pltpu.roll(values, shift % LON, 1)


def dot(a, b):
    return jnp.dot(a, b, preferred_element_type=F32)


def by_side(core, across, beside, use):
    pl.when(core[0] == 0)(lambda: use(across, beside) and None)
    pl.when(core[0] == 1)(lambda: use(beside, across) and None)


def split(total):
    high = total.astype(BF16)
    return high, (total - high.astype(F32)).astype(BF16)


def prepare_kernel(w1, w2, w1_out, w2_out, w_back):
    w1_out[...] = w1[...]
    w2_out[...] = w2[...]
    spare = jnp.zeros((C, VPAD - V), F32)
    for a in range(3):
        turned = []
        for b in range(3):
            tap = w2[:, (3 * a + b) * C : (3 * a + b + 1) * C].astype(F32)
            turned += [tap.T, spare]
        w_back[a] = jnp.concatenate(turned, axis=1).astype(BF16)


def forward_kernel(core, ends, across, local, beside, w1, w2, hidden, slope, outlook, sent, stack):
    wide = ROWS + 2

    def fill(chosen, ref):
        for a in range(3):
            for i in range(wide):
                if (i + a) // 2 == chosen:
                    row = ref[:, (i + a) % 2 * LON : ((i + a) % 2 + 1) * LON]
                    stack[a * C : (a + 1) * C, i * LON : (i + 1) * LON] = row

    fill(1, local)
    by_side(core, across, beside, lambda before, after: (fill(0, before), fill(2, after)))
    for i in range(wide):
        lanes = slice(i * LON, (i + 1) * LON)
        pre = None
        for b in range(3):
            taps = jnp.concatenate(
                [w1[:, (3 * a + b) * C : (3 * a + b + 1) * C] for a in range(3)], axis=1
            )
            part = turn(dot(taps, stack[:, lanes]), 1 - b)
            pre = part if pre is None else pre + part
        square = pre * pre
        t = jnp.tanh(GELU_A * pre * (1.0 + GELU_B * square))
        half = 0.5 * (1.0 + t)
        value = pre * half
        if i == 0:
            value = value * ends[0]
        if i == wide - 1:
            value = value * ends[1]
        hidden[:, lanes] = value.astype(BF16)
        if 0 < i < wide - 1:
            own = slice((i - 1) * LON, i * LON)
            slope[:, own] = half + (0.5 * GELU_A) * pre * (1.0 - t * t) * (
                1.0 + 3.0 * GELU_B * square
            )
    top = V // 16 * 16
    sent[top:, :] = jnp.zeros((MEMBERS * SHARE - top, CELLS), BF16)
    spare = jnp.zeros((VPAD - V, LON), F32)
    for i in range(ROWS):
        total = None
        for b in range(3):
            part = None
            for a in range(3):
                tap = w2[:, (3 * a + b) * C : (3 * a + b + 1) * C]
                term = dot(tap, hidden[:, (i + a) * LON : (i + a + 1) * LON])
                part = term if part is None else part + term
            part = turn(part, 1 - b)
            total = part if total is None else total + part
        lanes = slice(i * LON, (i + 1) * LON)
        outlook[:, lanes] = total
        sent[:VPAD, lanes] = jnp.concatenate([total, spare], axis=0).astype(BF16)


def score_kernel(points, me, every, obs, land, errors, loss):
    area = 1.0 + LAND_WEIGHT * land[...].astype(F32)
    x = [every[p].astype(F32) for p in range(MEMBERS)]
    truth = obs[me[0]]
    count = MEMBERS * (MEMBERS - 1)
    skill = pairs = jnp.zeros((SHARE, CELLS), F32)
    slopes = []
    for p in range(MEMBERS):
        d = x[p] - truth
        square = d * d + SOFTNESS * SOFTNESS
        inverse = lax.rsqrt(square)
        skill = skill + square * inverse
        slopes.append(d * inverse * (1.0 / MEMBERS))
    for p in range(MEMBERS):
        for q in range(p + 1, MEMBERS):
            d = x[p] - x[q]
            square = d * d + SOFTNESS * SOFTNESS
            inverse = lax.rsqrt(square)
            pairs = pairs + square * inverse
            s = d * inverse * (1.0 / count)
            slopes[p] = slopes[p] - s
            slopes[q] = slopes[q] + s
    variable = me[0] * SHARE + lax.broadcasted_iota(jnp.int32, (SHARE, CELLS), 0)
    crps = area * (skill * (1.0 / MEMBERS) - pairs * (1.0 / count))
    crps = jnp.where(variable < V, crps, 0.0)
    loss[...] = jnp.sum(crps, axis=(0, 1), keepdims=True) * (1.0 / points)
    factor = area * (LOSS_SCALE / points)
    for p in range(MEMBERS):
        errors[p] = (factor * slopes[p]).astype(BF16)


def backward_kernel(
    core, loss, err, err_across, err_beside, w_back, slope, hidden, across, local, beside, out, e, pg, ends
):
    def fill(i, row):
        row = row.astype(F32)
        for b in range(3):
            e[b * VPAD : (b + 1) * VPAD, i * LON : (i + 1) * LON] = turn(row, b - 1).astype(BF16)

    fill(1, err[:VPAD, :LON])
    fill(2, err[:VPAD, LON:])
    by_side(core, err_across, err_beside, lambda u, d: (fill(0, u[...]), fill(3, d[...])))

    def fill_ends(before, after):
        ends[:, :LON] = before[:, LON:]
        ends[:, LON:] = after[:, :LON]

    by_side(core, across, beside, fill_ends)
    for i in range(ROWS):
        back = None
        for a in range(3):
            start = (i + 2 - a) * LON
            term = dot(w_back[a], e[:, start : start + LON])
            back = term if back is None else back + term
        own = slice(i * LON, (i + 1) * LON)
        grad = back * slope[:, own]
        for b in range(3):
            pg[b * C : (b + 1) * C, own] = turn(grad, b - 1).astype(BF16)
    for a in range(3):
        if a == 0:
            window = jnp.concatenate([ends[:, :LON], local[:, :LON]], axis=1)
        elif a == 1:
            window = local[...]
        else:
            window = jnp.concatenate([local[:, LON:], ends[:, LON:]], axis=1)
        for b in range(3):
            first = lax.dot_general(
                pg[b * C : (b + 1) * C, :], window, NT, preferred_element_type=F32
            ).astype(BF16)
            second = lax.dot_general(
                e[b * VPAD : (b + 1) * VPAD, LON : 3 * LON],
                hidden[:, a * LON : a * LON + CELLS],
                NT,
                preferred_element_type=F32,
            ).astype(BF16)
            for part in range(2):
                tile = 2 * (3 * a + b) + part
                lanes = slice(part * LANES, (part + 1) * LANES)
                out[tile * C : (tile + 1) * C, :] = first[:, lanes]
                at = SECOND + tile * VPAD
                out[at : at + VPAD, :] = second[:, lanes]
    high, low = split(jnp.broadcast_to(loss[...], (1, LANES)))
    out[LOSS:, :] = jnp.zeros((FLAT - LOSS, LANES), BF16)
    row = lax.broadcasted_iota(jnp.int32, (16, LANES), 0)
    both = jnp.where(row == 0, high.astype(F32), jnp.where(row == 1, low.astype(F32), 0.0))
    out[LOSS : LOSS + 16, :] = both.astype(BF16)


def sum_kernel(row, holder, parts, out):
    total = parts[0].astype(F32)
    for i in range(1, parts.shape[0]):
        total = total + parts[i].astype(F32)
    copies = out.shape[0]
    value = total.astype(BF16)
    for i in range(copies):
        out[i] = value
    base = row // 16 * 16 if row + 16 <= total.shape[0] and row % 16 == 0 else 0
    span = 16 if row % 16 == 0 else total.shape[0]

    @pl.when(holder[0] == 1)
    def _():
        here = total[base : base + span]
        high, low = split(total[row : row + 1] + total[row + 1 : row + 2])
        index = lax.broadcasted_iota(jnp.int32, (span, LANES), 0) + base
        fixed = jnp.where(index == row, high.astype(F32), here)
        fixed = jnp.where(index == row + 1, low.astype(F32), fixed)
        for i in range(copies):
            out[i, base : base + span, :] = fixed.astype(BF16)


def summed(parts, row, holder, copies=1):
    body = lambda *refs: sum_kernel(row, *refs)
    return pl.pallas_call(
        body,
        out_shape=jax.ShapeDtypeStruct((copies,) + parts.shape[1:], BF16),
        in_specs=[SMEM, VMEM],
        out_specs=VMEM,
        compiler_params=PARAMS,
    )(holder, parts)


def last_kernel(sums, first, second, loss):
    for tile in range(TILES):
        lanes = slice(tile * LANES, (tile + 1) * LANES)
        first[:, lanes] = sums[tile * C : (tile + 1) * C, :]
        at = SECOND + tile * VPAD
        second[:, lanes] = sums[at : at + VPAD, :][:V]
    here = sums[LOSS : LOSS + 16, :].astype(F32)
    loss[...] = here[0:1, 0:1] + here[1:2, 0:1]


def exchange(array, axes):
    return lax.all_to_all(array, axes, 0, 0, tiled=True)


def body(features, w_first, later_kernel_matrix, observed_state, land):
    dom_size = lax.axis_size(DOM)
    dom = lax.axis_index(DOM)
    chips = [(i, i + 1) for i in range(1, dom_size - 1, 2)]
    chips += [(j, i) for i, j in chips]
    cores = [(i, i ^ 1) for i in range(dom_size)]
    side = lax.axis_index("c")
    core = side.reshape(1)
    points = float(V * ROWS * dom_size * LON)

    local = features.reshape(C, CELLS)
    across = lax.ppermute(local, DOM, chips)
    beside = lax.ppermute(local, DOM, cores)
    w1, w2, w_back = pl.pallas_call(
        prepare_kernel,
        out_shape=(
            jax.ShapeDtypeStruct((C, TAPS * C), BF16),
            jax.ShapeDtypeStruct((V, TAPS * C), BF16),
            jax.ShapeDtypeStruct((3, C, 3 * VPAD), BF16),
        ),
        in_specs=[VMEM] * 2,
        out_specs=(VMEM,) * 3,
        compiler_params=PARAMS,
    )(w_first, later_kernel_matrix)
    ends = jnp.stack([(dom > 0).astype(F32), (dom < dom_size - 1).astype(F32)])
    hidden, slope, outlook, sent = pl.pallas_call(
        forward_kernel,
        out_shape=(
            jax.ShapeDtypeStruct((C, 4 * LON), BF16),
            jax.ShapeDtypeStruct((C, CELLS), F32),
            jax.ShapeDtypeStruct((V, CELLS), F32),
            jax.ShapeDtypeStruct((MEMBERS * SHARE, CELLS), BF16),
        ),
        in_specs=[SMEM] * 2 + [VMEM] * 5,
        out_specs=(VMEM,) * 4,
        scratch_shapes=[pltpu.VMEM((3 * C, 4 * LON), BF16)],
        compiler_params=PARAMS,
    )(core, ends, across, local, beside, w1, w2)

    every = exchange(sent.reshape(MEMBERS, SHARE, CELLS), ENS)
    every, outlook = lax.optimization_barrier((every, outlook.reshape(1, V, ROWS, LON)))
    obs = jnp.pad(observed_state.reshape(V, CELLS), ((0, MEMBERS * SHARE - V), (0, 0)))
    me = lax.axis_index(ENS).reshape(1)
    errors, loss = pl.pallas_call(
        lambda *refs: score_kernel(points, *refs),
        out_shape=(
            jax.ShapeDtypeStruct((MEMBERS, SHARE, CELLS), BF16),
            jax.ShapeDtypeStruct((1, 1), F32),
        ),
        in_specs=[SMEM] + [VMEM] * 3,
        out_specs=(VMEM,) * 2,
        compiler_params=PARAMS,
    )(me, every, obs.reshape(MEMBERS, SHARE, CELLS), land.reshape(1, CELLS))
    errors = exchange(errors, ENS).reshape(MEMBERS * SHARE, CELLS)

    edge = lambda at: lax.dynamic_slice(errors, (0, at * LON), (VPAD, LON))
    err_across = lax.ppermute(edge(side), DOM, chips)
    err_beside = lax.ppermute(edge(1 - side), DOM, cores)
    flat = pl.pallas_call(
        backward_kernel,
        out_shape=jax.ShapeDtypeStruct((FLAT, LANES), BF16),
        in_specs=[SMEM] + [VMEM] * 10,
        out_specs=VMEM,
        scratch_shapes=[
            pltpu.VMEM((3 * VPAD, 4 * LON), BF16),
            pltpu.VMEM((3 * C, CELLS), BF16),
            pltpu.VMEM((C, CELLS), BF16),
        ],
        compiler_params=PARAMS,
    )(core, loss, errors, err_across, err_beside, w_back, slope, hidden, across, local, beside)

    holder = jnp.bool_(True)
    row = LOSS
    size = FLAT
    part = flat
    for axes, n in (("c", 2), ("x", 4), (Y, 8)):
        size //= n
        holder = holder & (lax.axis_index(axes) == row // size)
        row %= size
        part = exchange(part.reshape(n, size, LANES), axes)
        flag = holder.astype(jnp.int32).reshape(1)
        part = summed(part, row, flag, 8 if axes == Y else 1)
    part = summed(exchange(part, "z"), row, flag, 8)
    part = exchange(part, Y).reshape(8 * size, LANES)
    part = lax.all_gather(part, "x", axis=0, tiled=True)
    part = exchange(jnp.broadcast_to(part[None], (2, HALF, LANES)), "c").reshape(FLAT, LANES)
    first, second, loss = pl.pallas_call(
        last_kernel,
        out_shape=(
            jax.ShapeDtypeStruct((C, TAPS * C), BF16),
            jax.ShapeDtypeStruct((V, TAPS * C), BF16),
            jax.ShapeDtypeStruct((1, 1), F32),
        ),
        in_specs=[VMEM],
        out_specs=(VMEM,) * 3,
        compiler_params=PARAMS,
    )(part)
    return outlook, first, second, loss.reshape(())


def solution(mesh):
    split_mesh = Mesh(mesh.devices.reshape(tuple(PARTS.values())), tuple(PARTS))
    placed = (P(ENS, None, DOM, None), P(), P(), P(None, DOM, None), P(DOM, None))
    return jax.shard_map(
        body,
        mesh=split_mesh,
        in_specs=placed,
        out_specs=(P(ENS, None, DOM, None), P(), P(), P()),
        check_vma=False,
    )
```

```python
import jax
import jax.numpy as jnp
from jax import lax
from jax.experimental import pallas as pl
from jax.experimental.pallas import tpu as pltpu
from jax.sharding import Mesh
from jax.sharding import PartitionSpec as P

SOFTNESS = 0.25
LAND_WEIGHT = 2.0
LOSS_SCALE = 65536.0
GELU_A = 0.7978845608028654
GELU_B = 0.044715

ENS = ("x", "yh")
DOM = ("z", "yl", "c")
Y = ("yh", "yl")
PARTS = {"x": 4, "yh": 2, "z": 8, "yl": 4, "c": 2}
F32 = jnp.float32
BF16 = jnp.bfloat16

C = 256
V = 100
LON = 256
ROWS = 2
CELLS = ROWS * LON
MEMBERS = 8
SHARE = 16
VPAD = 112
TAPS = 9
LANES = 128
TILES = TAPS * C // LANES
SECOND = TILES * C
LOSS = SECOND + TILES * VPAD
FLAT = 6656
HALF = FLAT // 2
VMEM = pl.BlockSpec(memory_space=pltpu.VMEM)
SMEM = pl.BlockSpec(memory_space=pltpu.SMEM)
PARAMS = pltpu.CompilerParams(vmem_limit_bytes=40 * 1024 * 1024)
NT = (((1,), (1,)), ((), ()))


def turn(values, shift):
    return values if shift % LON == 0 else pltpu.roll(values, shift % LON, 1)


def dot(a, b):
    return jnp.dot(a, b, preferred_element_type=F32)


def by_side(core, across, beside, use):
    pl.when(core[0] == 0)(lambda: use(across, beside) and None)
    pl.when(core[0] == 1)(lambda: use(beside, across) and None)


def split(total):
    high = total.astype(BF16)
    return high, (total - high.astype(F32)).astype(BF16)


def prepare_kernel(w1, w2, w1_out, w2_out, w_back):
    w1_out[...] = w1[...]
    w2_out[...] = w2[...]
    spare = jnp.zeros((C, VPAD - V), F32)
    for a in range(3):
        turned = []
        for b in range(3):
            tap = w2[:, (3 * a + b) * C : (3 * a + b + 1) * C].astype(F32)
            turned += [tap.T, spare]
        w_back[a] = jnp.concatenate(turned, axis=1).astype(BF16)


def forward_kernel(core, ends, across, local, beside, w1, w2, hidden, slope, outlook, sent, stack):
    wide = ROWS + 2

    def fill(chosen, ref):
        for a in range(3):
            for i in range(wide):
                if (i + a) // 2 == chosen:
                    row = ref[:, (i + a) % 2 * LON : ((i + a) % 2 + 1) * LON]
                    stack[a * C : (a + 1) * C, i * LON : (i + 1) * LON] = row

    fill(1, local)
    by_side(core, across, beside, lambda before, after: (fill(0, before), fill(2, after)))
    for i in range(wide):
        lanes = slice(i * LON, (i + 1) * LON)
        pre = None
        for b in range(3):
            taps = jnp.concatenate(
                [w1[:, (3 * a + b) * C : (3 * a + b + 1) * C] for a in range(3)], axis=1
            )
            part = turn(dot(taps, stack[:, lanes]), 1 - b)
            pre = part if pre is None else pre + part
        square = pre * pre
        t = jnp.tanh(GELU_A * pre * (1.0 + GELU_B * square))
        half = 0.5 * (1.0 + t)
        value = pre * half
        if i == 0:
            value = value * ends[0]
        if i == wide - 1:
            value = value * ends[1]
        hidden[:, lanes] = value.astype(BF16)
        if 0 < i < wide - 1:
            own = slice((i - 1) * LON, i * LON)
            slope[:, own] = half + (0.5 * GELU_A) * pre * (1.0 - t * t) * (
                1.0 + 3.0 * GELU_B * square
            )
    top = V // 16 * 16
    sent[top:, :] = jnp.zeros((MEMBERS * SHARE - top, CELLS), BF16)
    spare = jnp.zeros((VPAD - V, LON), F32)
    for i in range(ROWS):
        total = None
        for b in range(3):
            part = None
            for a in range(3):
                tap = w2[:, (3 * a + b) * C : (3 * a + b + 1) * C]
                term = dot(tap, hidden[:, (i + a) * LON : (i + a + 1) * LON])
                part = term if part is None else part + term
            part = turn(part, 1 - b)
            total = part if total is None else total + part
        lanes = slice(i * LON, (i + 1) * LON)
        outlook[:, lanes] = total
        sent[:VPAD, lanes] = jnp.concatenate([total, spare], axis=0).astype(BF16)


def score_kernel(points, me, every, obs, land, errors, loss):
    area = 1.0 + LAND_WEIGHT * land[...].astype(F32)
    x = [every[p].astype(F32) for p in range(MEMBERS)]
    truth = obs[me[0]]
    count = MEMBERS * (MEMBERS - 1)
    skill = pairs = jnp.zeros((SHARE, CELLS), F32)
    slopes = []
    for p in range(MEMBERS):
        d = x[p] - truth
        square = d * d + SOFTNESS * SOFTNESS
        inverse = lax.rsqrt(square)
        skill = skill + square * inverse
        slopes.append(d * inverse * (1.0 / MEMBERS))
    for p in range(MEMBERS):
        for q in range(p + 1, MEMBERS):
            d = x[p] - x[q]
            square = d * d + SOFTNESS * SOFTNESS
            inverse = lax.rsqrt(square)
            pairs = pairs + square * inverse
            s = d * inverse * (1.0 / count)
            slopes[p] = slopes[p] - s
            slopes[q] = slopes[q] + s
    variable = me[0] * SHARE + lax.broadcasted_iota(jnp.int32, (SHARE, CELLS), 0)
    crps = area * (skill * (1.0 / MEMBERS) - pairs * (1.0 / count))
    crps = jnp.where(variable < V, crps, 0.0)
    loss[...] = jnp.sum(crps, axis=(0, 1), keepdims=True) * (1.0 / points)
    factor = area * (LOSS_SCALE / points)
    for p in range(MEMBERS):
        errors[p] = (factor * slopes[p]).astype(BF16)


def backward_kernel(
    core, loss, err, err_across, err_beside, w_back, slope, hidden, across, local, beside, out, e, pg, ends
):
    def fill(i, row):
        row = row.astype(F32)
        for b in range(3):
            e[b * VPAD : (b + 1) * VPAD, i * LON : (i + 1) * LON] = turn(row, b - 1).astype(BF16)

    fill(1, err[:VPAD, :LON])
    fill(2, err[:VPAD, LON:])
    by_side(core, err_across, err_beside, lambda u, d: (fill(0, u[...]), fill(3, d[...])))

    def fill_ends(before, after):
        ends[:, :LON] = before[:, LON:]
        ends[:, LON:] = after[:, :LON]

    by_side(core, across, beside, fill_ends)
    for i in range(ROWS):
        back = None
        for a in range(3):
            start = (i + 2 - a) * LON
            term = dot(w_back[a], e[:, start : start + LON])
            back = term if back is None else back + term
        own = slice(i * LON, (i + 1) * LON)
        grad = back * slope[:, own]
        for b in range(3):
            pg[b * C : (b + 1) * C, own] = turn(grad, b - 1).astype(BF16)
    for a in range(3):
        if a == 0:
            window = jnp.concatenate([ends[:, :LON], local[:, :LON]], axis=1)
        elif a == 1:
            window = local[...]
        else:
            window = jnp.concatenate([local[:, LON:], ends[:, LON:]], axis=1)
        for b in range(3):
            first = lax.dot_general(
                pg[b * C : (b + 1) * C, :], window, NT, preferred_element_type=F32
            ).astype(BF16)
            second = lax.dot_general(
                e[b * VPAD : (b + 1) * VPAD, LON : 3 * LON],
                hidden[:, a * LON : a * LON + CELLS],
                NT,
                preferred_element_type=F32,
            ).astype(BF16)
            for part in range(2):
                tile = 2 * (3 * a + b) + part
                lanes = slice(part * LANES, (part + 1) * LANES)
                out[tile * C : (tile + 1) * C, :] = first[:, lanes]
                at = SECOND + tile * VPAD
                out[at : at + VPAD, :] = second[:, lanes]
    high, low = split(jnp.broadcast_to(loss[...], (1, LANES)))
    out[LOSS:, :] = jnp.zeros((FLAT - LOSS, LANES), BF16)
    row = lax.broadcasted_iota(jnp.int32, (16, LANES), 0)
    both = jnp.where(row == 0, high.astype(F32), jnp.where(row == 1, low.astype(F32), 0.0))
    out[LOSS : LOSS + 16, :] = both.astype(BF16)


def sum_kernel(row, holder, parts, out):
    total = parts[0].astype(F32)
    for i in range(1, parts.shape[0]):
        total = total + parts[i].astype(F32)
    copies = out.shape[0]
    value = total.astype(BF16)
    for i in range(copies):
        out[i] = value
    base = row // 16 * 16 if row + 16 <= total.shape[0] and row % 16 == 0 else 0
    span = 16 if row % 16 == 0 else total.shape[0]

    @pl.when(holder[0] == 1)
    def _():
        here = total[base : base + span]
        high, low = split(total[row : row + 1] + total[row + 1 : row + 2])
        index = lax.broadcasted_iota(jnp.int32, (span, LANES), 0) + base
        fixed = jnp.where(index == row, high.astype(F32), here)
        fixed = jnp.where(index == row + 1, low.astype(F32), fixed)
        for i in range(copies):
            out[i, base : base + span, :] = fixed.astype(BF16)


def summed(parts, row, holder, copies=1):
    body = lambda *refs: sum_kernel(row, *refs)
    return pl.pallas_call(
        body,
        out_shape=jax.ShapeDtypeStruct((copies,) + parts.shape[1:], BF16),
        in_specs=[SMEM, VMEM],
        out_specs=VMEM,
        compiler_params=PARAMS,
    )(holder, parts)


def last_kernel(core, own, other, first, second, loss):
    def assemble(low, high):
        def flat(at, n):
            return low[at : at + n, :] if at < HALF else high[at - HALF : at - HALF + n, :]

        for tile in range(TILES):
            lanes = slice(tile * LANES, (tile + 1) * LANES)
            first[:, lanes] = flat(tile * C, C)
            second[:, lanes] = flat(SECOND + tile * VPAD, VPAD)[:V]
        here = flat(LOSS, 16).astype(F32)
        loss[...] = here[0:1, 0:1] + here[1:2, 0:1]

    pl.when(core[0] == 0)(lambda: assemble(own, other))
    pl.when(core[0] == 1)(lambda: assemble(other, own))


def exchange(array, axes):
    return lax.all_to_all(array, axes, 0, 0, tiled=True)


def body(features, w_first, later_kernel_matrix, observed_state, land):
    dom_size = lax.axis_size(DOM)
    dom = lax.axis_index(DOM)
    chips = [(i, i + 1) for i in range(1, dom_size - 1, 2)]
    chips += [(j, i) for i, j in chips]
    cores = [(i, i ^ 1) for i in range(dom_size)]
    side = lax.axis_index("c")
    core = side.reshape(1)
    points = float(V * ROWS * dom_size * LON)

    local = features.reshape(C, CELLS)
    across = lax.ppermute(local, DOM, chips)
    beside = lax.ppermute(local, DOM, cores)
    w1, w2, w_back = pl.pallas_call(
        prepare_kernel,
        out_shape=(
            jax.ShapeDtypeStruct((C, TAPS * C), BF16),
            jax.ShapeDtypeStruct((V, TAPS * C), BF16),
            jax.ShapeDtypeStruct((3, C, 3 * VPAD), BF16),
        ),
        in_specs=[VMEM] * 2,
        out_specs=(VMEM,) * 3,
        compiler_params=PARAMS,
    )(w_first, later_kernel_matrix)
    ends = jnp.stack([(dom > 0).astype(F32), (dom < dom_size - 1).astype(F32)])
    obs = jnp.pad(observed_state.reshape(V, CELLS), ((0, MEMBERS * SHARE - V), (0, 0)))
    obs = obs.reshape(MEMBERS, SHARE, CELLS)
    area = land.reshape(1, CELLS)
    me = lax.axis_index(ENS).reshape(1)
    upper = side == 0
    across, obs, area, me, upper, ends = lax.optimization_barrier(
        (across, obs, area, me, upper, ends)
    )
    hidden, slope, outlook, sent = pl.pallas_call(
        forward_kernel,
        out_shape=(
            jax.ShapeDtypeStruct((C, 4 * LON), BF16),
            jax.ShapeDtypeStruct((C, CELLS), F32),
            jax.ShapeDtypeStruct((V, CELLS), F32),
            jax.ShapeDtypeStruct((MEMBERS * SHARE, CELLS), BF16),
        ),
        in_specs=[SMEM] * 2 + [VMEM] * 5,
        out_specs=(VMEM,) * 4,
        scratch_shapes=[pltpu.VMEM((3 * C, 4 * LON), BF16)],
        compiler_params=PARAMS,
    )(core, ends, across, local, beside, w1, w2)

    every = exchange(sent.reshape(MEMBERS, SHARE, CELLS), ENS)
    errors, loss = pl.pallas_call(
        lambda *refs: score_kernel(points, *refs),
        out_shape=(
            jax.ShapeDtypeStruct((MEMBERS, SHARE, CELLS), BF16),
            jax.ShapeDtypeStruct((1, 1), F32),
        ),
        in_specs=[SMEM] + [VMEM] * 3,
        out_specs=(VMEM,) * 2,
        compiler_params=PARAMS,
    )(me, every, obs, area)
    errors = exchange(errors, ENS).reshape(MEMBERS * SHARE, CELLS)

    first, last = errors[:VPAD, :LON], errors[:VPAD, LON:]
    err_across = lax.ppermute(jnp.where(upper, first, last), DOM, chips)
    err_beside = lax.ppermute(jnp.where(upper, last, first), DOM, cores)
    outlook = outlook.reshape(1, V, ROWS, LON)
    err_across, outlook = lax.optimization_barrier((err_across, outlook))
    flat = pl.pallas_call(
        backward_kernel,
        out_shape=jax.ShapeDtypeStruct((FLAT, LANES), BF16),
        in_specs=[SMEM] + [VMEM] * 10,
        out_specs=VMEM,
        scratch_shapes=[
            pltpu.VMEM((3 * VPAD, 4 * LON), BF16),
            pltpu.VMEM((3 * C, CELLS), BF16),
            pltpu.VMEM((C, CELLS), BF16),
        ],
        compiler_params=PARAMS,
    )(core, loss, errors, err_across, err_beside, w_back, slope, hidden, across, local, beside)

    stages = (("c", 2), ("x", 4), (Y, 8))
    holder = jnp.bool_(True)
    row, size = LOSS, FLAT
    flags, places = [], []
    for axes, n in stages:
        size //= n
        holder = holder & (lax.axis_index(axes) == row // size)
        row %= size
        flags.append(holder.astype(jnp.int32).reshape(1))
        places.append((row, size))
    part, flags = lax.optimization_barrier((flat, flags))
    for (axes, n), flag, (row, size) in zip(stages, flags, places):
        part = exchange(part.reshape(n, size, LANES), axes)
        part = summed(part, row, flag, 8 if axes == Y else 1)
    part = summed(exchange(part, "z"), row, flag, 8)
    part = exchange(part, Y).reshape(8 * size, LANES)
    part = lax.all_gather(part, "x", axis=0, tiled=True)
    other = lax.ppermute(part, "c", [(0, 1), (1, 0)])
    first, second, loss = pl.pallas_call(
        last_kernel,
        out_shape=(
            jax.ShapeDtypeStruct((C, TAPS * C), BF16),
            jax.ShapeDtypeStruct((V, TAPS * C), BF16),
            jax.ShapeDtypeStruct((1, 1), F32),
        ),
        in_specs=[SMEM, VMEM, VMEM],
        out_specs=(VMEM,) * 3,
        compiler_params=PARAMS,
    )(core, part, other)
    return outlook, first, second, loss.reshape(())


def solution(mesh):
    split_mesh = Mesh(mesh.devices.reshape(tuple(PARTS.values())), tuple(PARTS))
    placed = (P(ENS, None, DOM, None), P(), P(), P(None, DOM, None), P(DOM, None))
    return jax.shard_map(
        body,
        mesh=split_mesh,
        in_specs=placed,
        out_specs=(P(ENS, None, DOM, None), P(), P(), P()),
        check_vma=False,
    )
```

```python
import jax
import jax.numpy as jnp
from jax import lax
from jax.experimental import pallas as pl
from jax.experimental.pallas import tpu as pltpu
from jax.sharding import Mesh
from jax.sharding import PartitionSpec as P

SOFTNESS = 0.25
LAND_WEIGHT = 2.0
LOSS_SCALE = 65536.0
GELU_A = 0.7978845608028654
GELU_B = 0.044715

ENS = ("x", "yh")
DOM = ("z", "yl", "c")
Y = ("yh", "yl")
PARTS = {"x": 4, "yh": 2, "z": 8, "yl": 4, "c": 2}
F32 = jnp.float32
BF16 = jnp.bfloat16

C = 256
V = 100
LON = 256
ROWS = 2
CELLS = ROWS * LON
MEMBERS = 8
SHARE = 16
VPAD = 112
TAPS = 9
LANES = 128
TILES = TAPS * C // LANES
SECOND = TILES * C
LOSS = SECOND + TILES * VPAD
FLAT = 6656
HALF = FLAT // 2
VMEM = pl.BlockSpec(memory_space=pltpu.VMEM)
SMEM = pl.BlockSpec(memory_space=pltpu.SMEM)
PARAMS = pltpu.CompilerParams(vmem_limit_bytes=40 * 1024 * 1024)
NT = (((1,), (1,)), ((), ()))


def turn(values, shift):
    return values if shift % LON == 0 else pltpu.roll(values, shift % LON, 1)


def dot(a, b):
    return jnp.dot(a, b, preferred_element_type=F32)


def by_side(core, across, beside, use):
    pl.when(core[0] == 0)(lambda: use(across, beside) and None)
    pl.when(core[0] == 1)(lambda: use(beside, across) and None)


def split(total):
    high = total.astype(BF16)
    return high, (total - high.astype(F32)).astype(BF16)


def prepare_kernel(w1, w2, w1_out, w2_out, w_back):
    w1_out[...] = w1[...]
    w2_out[...] = w2[...]
    spare = jnp.zeros((C, VPAD - V), F32)
    for a in range(3):
        turned = []
        for b in range(3):
            tap = w2[:, (3 * a + b) * C : (3 * a + b + 1) * C].astype(F32)
            turned += [tap.T, spare]
        w_back[a] = jnp.concatenate(turned, axis=1).astype(BF16)


def forward_kernel(core, ends, across, local, beside, w1, w2, hidden, slope, outlook, sent, stack):
    wide = ROWS + 2

    def fill(chosen, ref):
        for a in range(3):
            for i in range(wide):
                if (i + a) // 2 == chosen:
                    row = ref[:, (i + a) % 2 * LON : ((i + a) % 2 + 1) * LON]
                    stack[a * C : (a + 1) * C, i * LON : (i + 1) * LON] = row

    fill(1, local)
    by_side(core, across, beside, lambda before, after: (fill(0, before), fill(2, after)))
    for i in range(wide):
        lanes = slice(i * LON, (i + 1) * LON)
        pre = None
        for b in range(3):
            taps = jnp.concatenate(
                [w1[:, (3 * a + b) * C : (3 * a + b + 1) * C] for a in range(3)], axis=1
            )
            part = turn(dot(taps, stack[:, lanes]), 1 - b)
            pre = part if pre is None else pre + part
        square = pre * pre
        t = jnp.tanh(GELU_A * pre * (1.0 + GELU_B * square))
        half = 0.5 * (1.0 + t)
        value = pre * half
        if i == 0:
            value = value * ends[0]
        if i == wide - 1:
            value = value * ends[1]
        hidden[:, lanes] = value.astype(BF16)
        steep = half + (0.5 * GELU_A) * pre * (1.0 - t * t) * (1.0 + 3.0 * GELU_B * square)
        if i == 0:
            steep = steep * ends[0]
        if i == wide - 1:
            steep = steep * ends[1]
        slope[:, lanes] = steep
    top = V // 16 * 16
    sent[top:, :] = jnp.zeros((MEMBERS * SHARE - top, CELLS), BF16)
    spare = jnp.zeros((VPAD - V, LON), F32)
    for i in range(ROWS):
        total = None
        for b in range(3):
            part = None
            for a in range(3):
                tap = w2[:, (3 * a + b) * C : (3 * a + b + 1) * C]
                term = dot(tap, hidden[:, (i + a) * LON : (i + a + 1) * LON])
                part = term if part is None else part + term
            part = turn(part, 1 - b)
            total = part if total is None else total + part
        lanes = slice(i * LON, (i + 1) * LON)
        outlook[:, lanes] = total
        sent[:VPAD, lanes] = jnp.concatenate([total, spare], axis=0).astype(BF16)


def score_kernel(points, me, every, obs, land, errors, loss):
    area = 1.0 + LAND_WEIGHT * land[...].astype(F32)
    x = [every[p].astype(F32) for p in range(MEMBERS)]
    truth = obs[me[0]]
    count = MEMBERS * (MEMBERS - 1)
    skill = pairs = jnp.zeros((SHARE, CELLS), F32)
    slopes = []
    for p in range(MEMBERS):
        d = x[p] - truth
        square = d * d + SOFTNESS * SOFTNESS
        inverse = lax.rsqrt(square)
        skill = skill + square * inverse
        slopes.append(d * inverse * (1.0 / MEMBERS))
    for p in range(MEMBERS):
        for q in range(p + 1, MEMBERS):
            d = x[p] - x[q]
            square = d * d + SOFTNESS * SOFTNESS
            inverse = lax.rsqrt(square)
            pairs = pairs + square * inverse
            s = d * inverse * (1.0 / count)
            slopes[p] = slopes[p] - s
            slopes[q] = slopes[q] + s
    variable = me[0] * SHARE + lax.broadcasted_iota(jnp.int32, (SHARE, CELLS), 0)
    crps = area * (skill * (1.0 / MEMBERS) - pairs * (1.0 / count))
    crps = jnp.where(variable < V, crps, 0.0)
    loss[...] = jnp.sum(crps, axis=(0, 1), keepdims=True) * (1.0 / points)
    factor = area * (LOSS_SCALE / points)
    for p in range(MEMBERS):
        errors[p] = (factor * slopes[p]).astype(BF16)


def backward_kernel(
    core, loss, err, w_back, slope, hidden, across, local, beside, out, e, pg, trunk
):
    trunk[:, 2 * LON : 4 * LON] = local[...]

    def fill(before, after):
        trunk[:, : 2 * LON] = before[...]
        trunk[:, 4 * LON :] = after[...]

    by_side(core, across, beside, fill)
    for i in range(ROWS):
        row = err[:VPAD, i * LON : (i + 1) * LON].astype(F32)
        for b in range(3):
            e[b * VPAD : (b + 1) * VPAD, i * LON : (i + 1) * LON] = turn(row, b - 1).astype(BF16)
    wide = ROWS + 2
    for i in range(wide):
        back = None
        for a in range(3):
            if 0 <= i - a < ROWS:
                term = dot(w_back[a], e[:, (i - a) * LON : (i - a + 1) * LON])
                back = term if back is None else back + term
        lanes = slice(i * LON, (i + 1) * LON)
        grad = back * slope[:, lanes]
        for b in range(3):
            pg[b * C : (b + 1) * C, lanes] = turn(grad, b - 1).astype(BF16)
    for a in range(3):
        window = trunk[:, a * LON : (a + wide) * LON]
        for b in range(3):
            first = lax.dot_general(
                pg[b * C : (b + 1) * C, :], window, NT, preferred_element_type=F32
            ).astype(BF16)
            second = lax.dot_general(
                e[b * VPAD : (b + 1) * VPAD, :],
                hidden[:, a * LON : a * LON + CELLS],
                NT,
                preferred_element_type=F32,
            ).astype(BF16)
            for part in range(2):
                tile = 2 * (3 * a + b) + part
                lanes = slice(part * LANES, (part + 1) * LANES)
                out[tile * C : (tile + 1) * C, :] = first[:, lanes]
                at = SECOND + tile * VPAD
                out[at : at + VPAD, :] = second[:, lanes]
    high, low = split(jnp.broadcast_to(loss[...], (1, LANES)))
    out[LOSS:, :] = jnp.zeros((FLAT - LOSS, LANES), BF16)
    row = lax.broadcasted_iota(jnp.int32, (16, LANES), 0)
    both = jnp.where(row == 0, high.astype(F32), jnp.where(row == 1, low.astype(F32), 0.0))
    out[LOSS : LOSS + 16, :] = both.astype(BF16)


def sum_kernel(row, holder, parts, out):
    total = parts[0].astype(F32)
    for i in range(1, parts.shape[0]):
        total = total + parts[i].astype(F32)
    copies = out.shape[0]
    value = total.astype(BF16)
    for i in range(copies):
        out[i] = value
    base = row // 16 * 16 if row + 16 <= total.shape[0] and row % 16 == 0 else 0
    span = 16 if row % 16 == 0 else total.shape[0]

    @pl.when(holder[0] == 1)
    def _():
        here = total[base : base + span]
        high, low = split(total[row : row + 1] + total[row + 1 : row + 2])
        index = lax.broadcasted_iota(jnp.int32, (span, LANES), 0) + base
        fixed = jnp.where(index == row, high.astype(F32), here)
        fixed = jnp.where(index == row + 1, low.astype(F32), fixed)
        for i in range(copies):
            out[i, base : base + span, :] = fixed.astype(BF16)


def summed(parts, row, holder, copies=1):
    body = lambda *refs: sum_kernel(row, *refs)
    return pl.pallas_call(
        body,
        out_shape=jax.ShapeDtypeStruct((copies,) + parts.shape[1:], BF16),
        in_specs=[SMEM, VMEM],
        out_specs=VMEM,
        compiler_params=PARAMS,
    )(holder, parts)


def last_kernel(core, own, other, first, second, loss):
    def assemble(low, high):
        def flat(at, n):
            return low[at : at + n, :] if at < HALF else high[at - HALF : at - HALF + n, :]

        for tile in range(TILES):
            lanes = slice(tile * LANES, (tile + 1) * LANES)
            first[:, lanes] = flat(tile * C, C)
            second[:, lanes] = flat(SECOND + tile * VPAD, VPAD)[:V]
        here = flat(LOSS, 16).astype(F32)
        loss[...] = here[0:1, 0:1] + here[1:2, 0:1]

    pl.when(core[0] == 0)(lambda: assemble(own, other))
    pl.when(core[0] == 1)(lambda: assemble(other, own))


def exchange(array, axes):
    return lax.all_to_all(array, axes, 0, 0, tiled=True)


def body(features, w_first, later_kernel_matrix, observed_state, land):
    dom_size = lax.axis_size(DOM)
    dom = lax.axis_index(DOM)
    chips = [(i, i + 1) for i in range(1, dom_size - 1, 2)]
    chips += [(j, i) for i, j in chips]
    cores = [(i, i ^ 1) for i in range(dom_size)]
    side = lax.axis_index("c")
    core = side.reshape(1)
    points = float(V * ROWS * dom_size * LON)

    local = features.reshape(C, CELLS)
    across = lax.ppermute(local, DOM, chips)
    beside = lax.ppermute(local, DOM, cores)
    w1, w2, w_back = pl.pallas_call(
        prepare_kernel,
        out_shape=(
            jax.ShapeDtypeStruct((C, TAPS * C), BF16),
            jax.ShapeDtypeStruct((V, TAPS * C), BF16),
            jax.ShapeDtypeStruct((3, C, 3 * VPAD), BF16),
        ),
        in_specs=[VMEM] * 2,
        out_specs=(VMEM,) * 3,
        compiler_params=PARAMS,
    )(w_first, later_kernel_matrix)
    ends = jnp.stack([(dom > 0).astype(F32), (dom < dom_size - 1).astype(F32)])
    obs = jnp.pad(observed_state.reshape(V, CELLS), ((0, MEMBERS * SHARE - V), (0, 0)))
    obs = obs.reshape(MEMBERS, SHARE, CELLS)
    area = land.reshape(1, CELLS)
    me = lax.axis_index(ENS).reshape(1)
    stages = (("c", 2), ("x", 4), (Y, 8))
    holder = jnp.bool_(True)
    row, size = LOSS, FLAT
    flags, places = [], []
    for axes, n in stages:
        size //= n
        holder = holder & (lax.axis_index(axes) == row // size)
        row %= size
        flags.append(holder.astype(jnp.int32).reshape(1))
        places.append((row, size))
    across, obs, area, me, ends, flags = lax.optimization_barrier(
        (across, obs, area, me, ends, flags)
    )
    hidden, slope, outlook, sent = pl.pallas_call(
        forward_kernel,
        out_shape=(
            jax.ShapeDtypeStruct((C, 4 * LON), BF16),
            jax.ShapeDtypeStruct((C, 4 * LON), F32),
            jax.ShapeDtypeStruct((V, CELLS), F32),
            jax.ShapeDtypeStruct((MEMBERS * SHARE, CELLS), BF16),
        ),
        in_specs=[SMEM] * 2 + [VMEM] * 5,
        out_specs=(VMEM,) * 4,
        scratch_shapes=[pltpu.VMEM((3 * C, 4 * LON), BF16)],
        compiler_params=PARAMS,
    )(core, ends, across, local, beside, w1, w2)

    every = exchange(sent.reshape(MEMBERS, SHARE, CELLS), ENS)
    errors, loss = pl.pallas_call(
        lambda *refs: score_kernel(points, *refs),
        out_shape=(
            jax.ShapeDtypeStruct((MEMBERS, SHARE, CELLS), BF16),
            jax.ShapeDtypeStruct((1, 1), F32),
        ),
        in_specs=[SMEM] + [VMEM] * 3,
        out_specs=(VMEM,) * 2,
        compiler_params=PARAMS,
    )(me, every, obs, area)
    errors = exchange(errors, ENS).reshape(MEMBERS * SHARE, CELLS)

    flat = pl.pallas_call(
        backward_kernel,
        out_shape=jax.ShapeDtypeStruct((FLAT, LANES), BF16),
        in_specs=[SMEM] + [VMEM] * 8,
        out_specs=VMEM,
        scratch_shapes=[
            pltpu.VMEM((3 * VPAD, CELLS), BF16),
            pltpu.VMEM((3 * C, 4 * LON), BF16),
            pltpu.VMEM((C, 6 * LON), BF16),
        ],
        compiler_params=PARAMS,
    )(core, loss, errors, w_back, slope, hidden, across, local, beside)

    part = flat
    for (axes, n), flag, (row, size) in zip(stages, flags, places):
        part = exchange(part.reshape(n, size, LANES), axes)
        part = summed(part, row, flag, 8 if axes == Y else 1)
    part = summed(exchange(part, "z"), row, flag, 8)
    part = exchange(part, Y).reshape(8 * size, LANES)
    part = lax.all_gather(part, "x", axis=0, tiled=True)
    other = lax.ppermute(part, "c", [(0, 1), (1, 0)])
    other, outlook = lax.optimization_barrier((other, outlook.reshape(1, V, ROWS, LON)))
    first, second, loss = pl.pallas_call(
        last_kernel,
        out_shape=(
            jax.ShapeDtypeStruct((C, TAPS * C), BF16),
            jax.ShapeDtypeStruct((V, TAPS * C), BF16),
            jax.ShapeDtypeStruct((1, 1), F32),
        ),
        in_specs=[SMEM, VMEM, VMEM],
        out_specs=(VMEM,) * 3,
        compiler_params=PARAMS,
    )(core, part, other)
    return outlook, first, second, loss.reshape(())


def solution(mesh):
    split_mesh = Mesh(mesh.devices.reshape(tuple(PARTS.values())), tuple(PARTS))
    placed = (P(ENS, None, DOM, None), P(), P(), P(None, DOM, None), P(DOM, None))
    return jax.shard_map(
        body,
        mesh=split_mesh,
        in_specs=placed,
        out_specs=(P(ENS, None, DOM, None), P(), P(), P()),
        check_vma=False,
    )
```

```python
import jax
import jax.numpy as jnp
from jax import lax
from jax.experimental import pallas as pl
from jax.experimental.pallas import tpu as pltpu
from jax.sharding import Mesh
from jax.sharding import PartitionSpec as P

SOFTNESS = 0.25
LAND_WEIGHT = 2.0
LOSS_SCALE = 65536.0
GELU_A = 0.7978845608028654
GELU_B = 0.044715

ENS = ("x", "yh")
DOM = ("z", "yl", "c")
Y = ("yh", "yl")
PARTS = {"x": 4, "yh": 2, "z": 8, "yl": 4, "c": 2}
F32 = jnp.float32
BF16 = jnp.bfloat16

C = 256
V = 100
LON = 256
ROWS = 2
CELLS = ROWS * LON
MEMBERS = 8
FIRST = 48
SHARE = 56
VPAD = 112
TAPS = 9
LANES = 128
TILES = TAPS * C // LANES
SECOND = TILES * C
LOSS = SECOND + TILES * VPAD
FLAT = 6656
HALF = FLAT // 2
VMEM = pl.BlockSpec(memory_space=pltpu.VMEM)
SMEM = pl.BlockSpec(memory_space=pltpu.SMEM)
PARAMS = pltpu.CompilerParams(vmem_limit_bytes=40 * 1024 * 1024)
NT = (((1,), (1,)), ((), ()))


def turn(values, shift):
    return values if shift % LON == 0 else pltpu.roll(values, shift % LON, 1)


def dot(a, b):
    return jnp.dot(a, b, preferred_element_type=F32)


def by_side(core, across, beside, use):
    pl.when(core[0] == 0)(lambda: use(across, beside) and None)
    pl.when(core[0] == 1)(lambda: use(beside, across) and None)


def split(total):
    high = total.astype(BF16)
    return high, (total - high.astype(F32)).astype(BF16)


def prepare_kernel(w1, w2, w1_out, w2_out, w_back):
    w1_out[...] = w1[...]
    w2_out[...] = w2[...]
    spare = jnp.zeros((C, VPAD - V), F32)
    for a in range(3):
        turned = []
        for b in range(3):
            tap = w2[:, (3 * a + b) * C : (3 * a + b + 1) * C].astype(F32)
            turned += [tap.T, spare]
        w_back[a] = jnp.concatenate(turned, axis=1).astype(BF16)


def forward_kernel(core, ends, across, local, beside, w1, w2, hidden, slope, outlook, sent, stack):
    wide = ROWS + 2

    def fill(chosen, ref):
        for a in range(3):
            for i in range(wide):
                if (i + a) // 2 == chosen:
                    row = ref[:, (i + a) % 2 * LON : ((i + a) % 2 + 1) * LON]
                    stack[a * C : (a + 1) * C, i * LON : (i + 1) * LON] = row

    fill(1, local)
    by_side(core, across, beside, lambda before, after: (fill(0, before), fill(2, after)))
    for i in range(wide):
        lanes = slice(i * LON, (i + 1) * LON)
        pre = None
        for b in range(3):
            taps = jnp.concatenate(
                [w1[:, (3 * a + b) * C : (3 * a + b + 1) * C] for a in range(3)], axis=1
            )
            part = turn(dot(taps, stack[:, lanes]), 1 - b)
            pre = part if pre is None else pre + part
        square = pre * pre
        t = jnp.tanh(GELU_A * pre * (1.0 + GELU_B * square))
        half = 0.5 * (1.0 + t)
        value = pre * half
        if i == 0:
            value = value * ends[0]
        if i == wide - 1:
            value = value * ends[1]
        hidden[:, lanes] = value.astype(BF16)
        steep = half + (0.5 * GELU_A) * pre * (1.0 - t * t) * (1.0 + 3.0 * GELU_B * square)
        if i == 0:
            steep = steep * ends[0]
        if i == wide - 1:
            steep = steep * ends[1]
        slope[:, lanes] = steep
    spare = jnp.zeros((FIRST + SHARE - V, LON), F32)
    for i in range(ROWS):
        total = None
        for b in range(3):
            part = None
            for a in range(3):
                tap = w2[:, (3 * a + b) * C : (3 * a + b + 1) * C]
                term = dot(tap, hidden[:, (i + a) * LON : (i + a + 1) * LON])
                part = term if part is None else part + term
            part = turn(part, 1 - b)
            total = part if total is None else total + part
        lanes = slice(i * LON, (i + 1) * LON)
        outlook[:, lanes] = total
        padded = jnp.concatenate([total, spare], axis=0)
        for part in range(2):
            tile = padded[:, part * LANES : (part + 1) * LANES]
            sent[2 * i + part] = tile[:SHARE].astype(BF16)
            sent[4 + 2 * i + part] = tile[FIRST:].astype(BF16)


def score_kernel(points, me, every, obs, land, errors, loss):
    half = me[0] // 4
    cells = pl.ds(pl.multiple_of(me[0] % 4 * LANES, LANES), LANES)
    area = 1.0 + LAND_WEIGHT * land[:, cells].astype(F32)
    x = [every[p].astype(F32) for p in range(MEMBERS)]
    truth = obs[pl.ds(pl.multiple_of(half * FIRST, FIRST), SHARE), cells]
    count = MEMBERS * (MEMBERS - 1)
    skill = pairs = jnp.zeros((SHARE, LANES), F32)
    slopes = []
    for p in range(MEMBERS):
        d = x[p] - truth
        square = d * d + SOFTNESS * SOFTNESS
        inverse = lax.rsqrt(square)
        skill = skill + square * inverse
        slopes.append(d * inverse * (1.0 / MEMBERS))
    for p in range(MEMBERS):
        for q in range(p + 1, MEMBERS):
            d = x[p] - x[q]
            square = d * d + SOFTNESS * SOFTNESS
            inverse = lax.rsqrt(square)
            pairs = pairs + square * inverse
            s = d * inverse * (1.0 / count)
            slopes[p] = slopes[p] - s
            slopes[q] = slopes[q] + s
    variable = lax.broadcasted_iota(jnp.int32, (SHARE, LANES), 0)
    crps = area * (skill * (1.0 / MEMBERS) - pairs * (1.0 / count))
    crps = jnp.where(variable < jnp.where(half == 0, FIRST, V - FIRST), crps, 0.0)
    loss[...] = jnp.sum(crps, axis=(0, 1), keepdims=True) * (1.0 / points)
    factor = area * (LOSS_SCALE / points)
    for p in range(MEMBERS):
        errors[p] = (factor * slopes[p]).astype(BF16)


def backward_kernel(
    core, loss, err, w_back, slope, hidden, across, local, beside, theirs, e, pg, trunk
):
    trunk[:, 2 * LON : 4 * LON] = local[...]

    def fill(before, after):
        trunk[:, : 2 * LON] = before[...]
        trunk[:, 4 * LON :] = after[...]

    by_side(core, across, beside, fill)
    for i in range(ROWS):
        spare = jnp.zeros((VPAD - FIRST - SHARE, LANES), F32)
        tiles = []
        for tile in (2 * i, 2 * i + 1):
            lower, upper = err[tile].astype(F32)[:FIRST], err[4 + tile].astype(F32)
            tiles.append(jnp.concatenate([lower, upper, spare], axis=0))
        row = jnp.concatenate(tiles, axis=1)
        for b in range(3):
            e[b * VPAD : (b + 1) * VPAD, i * LON : (i + 1) * LON] = turn(row, b - 1).astype(BF16)
    wide = ROWS + 2
    for i in range(wide):
        back = None
        for a in range(3):
            if 0 <= i - a < ROWS:
                term = dot(w_back[a], e[:, (i - a) * LON : (i - a + 1) * LON])
                back = term if back is None else back + term
        lanes = slice(i * LON, (i + 1) * LON)
        grad = back * slope[:, lanes]
        for b in range(3):
            pg[b * C : (b + 1) * C, lanes] = turn(grad, b - 1).astype(BF16)
    pl.when(core[0] == 0)(lambda: lower_half(loss, hidden, e, pg, trunk, theirs))
    pl.when(core[0] == 1)(lambda: upper_half(pg, trunk, theirs))


def own_half_kernel(core, loss, hidden, e, pg, trunk, mine):
    pl.when(core[0] == 0)(lambda: upper_half(pg, trunk, mine))
    pl.when(core[0] == 1)(lambda: lower_half(loss, hidden, e, pg, trunk, mine))


def first_tiles(pg, trunk, tiles, out, start):
    a = tiles[0] // 6
    window = trunk[:, a * LON : (a + ROWS + 2) * LON]
    head, tail = tiles[0] % 6 // 2, tiles[-1] % 6 // 2
    both = lax.dot_general(
        pg[head * C : (tail + 1) * C, :], window, NT, preferred_element_type=F32
    )
    for tile in tiles:
        b, part = tile % 6 // 2 - head, tile % 2
        value = both[b * C : (b + 1) * C, part * LANES : (part + 1) * LANES]
        out[tile * C - start : (tile + 1) * C - start, :] = value.astype(BF16)


def upper_half(pg, trunk, out):
    for tiles in (range(6), range(6, 12), range(12, 13)):
        first_tiles(pg, trunk, tiles, out, 0)


def lower_half(loss, hidden, e, pg, trunk, out):
    first_tiles(pg, trunk, range(13, 18), out, HALF)
    for a in range(3):
        reach = hidden[:, a * LON : a * LON + CELLS]
        seconds = lax.dot_general(e[...], reach, NT, preferred_element_type=F32)
        for b in range(3):
            second = seconds[b * VPAD : (b + 1) * VPAD].astype(BF16)
            for part in range(2):
                at = SECOND + (2 * (3 * a + b) + part) * VPAD - HALF
                out[at : at + VPAD, :] = second[:, part * LANES : (part + 1) * LANES]
    high, low = split(jnp.broadcast_to(loss[...], (1, LANES)))
    index = lax.broadcasted_iota(jnp.int32, (16, LANES), 0)
    both = jnp.where(index == 0, high.astype(F32), jnp.where(index == 1, low.astype(F32), 0.0))
    at = LOSS - HALF
    out[at : at + 16, :] = both.astype(BF16)
    out[at + 16 :, :] = jnp.zeros((HALF - at - 16, LANES), BF16)


def sum_kernel(row, holder, *refs):
    out = refs[-1]

    def total(at, n):
        value = None
        for parts in refs[:-1]:
            for i in range(parts.shape[0]):
                term = parts[i, at : at + n].astype(F32)
                value = term if value is None else value + term
        return value

    copies, size = out.shape[:2]
    value = total(0, size).astype(BF16)
    for i in range(copies):
        out[i] = value
    base, span = (row, 16) if row % 16 == 0 else (0, size)

    @pl.when(holder[0] == 1)
    def _():
        here = total(base, span)
        high, low = split(here[row - base : row - base + 1] + here[row - base + 1 : row - base + 2])
        index = lax.broadcasted_iota(jnp.int32, (span, LANES), 0) + base
        fixed = jnp.where(index == row, high.astype(F32), here)
        fixed = jnp.where(index == row + 1, low.astype(F32), fixed)
        for i in range(copies):
            out[i, base : base + span, :] = fixed.astype(BF16)


def summed(row, holder, copies, *arrays):
    body = lambda *refs: sum_kernel(row, *refs)
    return pl.pallas_call(
        body,
        out_shape=jax.ShapeDtypeStruct((copies,) + arrays[0].shape[1:], BF16),
        in_specs=[SMEM] + [VMEM] * len(arrays),
        out_specs=VMEM,
        compiler_params=PARAMS,
    )(holder, *arrays)


def last_kernel(core, own, other, first, second, loss):
    def assemble(low, high):
        def flat(at, n):
            return low[at : at + n, :] if at < HALF else high[at - HALF : at - HALF + n, :]

        for tile in range(TILES):
            lanes = slice(tile * LANES, (tile + 1) * LANES)
            first[:, lanes] = flat(tile * C, C)
            second[:, lanes] = flat(SECOND + tile * VPAD, VPAD)[:V]
        here = flat(LOSS, 16).astype(F32)
        loss[...] = here[0:1, 0:1] + here[1:2, 0:1]

    pl.when(core[0] == 0)(lambda: assemble(own, other))
    pl.when(core[0] == 1)(lambda: assemble(other, own))


def exchange(array, axes):
    return lax.all_to_all(array, axes, 0, 0, tiled=True)


def body(features, w_first, later_kernel_matrix, observed_state, land):
    dom_size = lax.axis_size(DOM)
    dom = lax.axis_index(DOM)
    chips = [(i, i + 1) for i in range(1, dom_size - 1, 2)]
    chips += [(j, i) for i, j in chips]
    cores = [(i, i ^ 1) for i in range(dom_size)]
    side = lax.axis_index("c")
    core = side.reshape(1)
    points = float(V * ROWS * dom_size * LON)

    local = features.reshape(C, CELLS)
    across = lax.ppermute(local, DOM, chips)
    beside = lax.ppermute(local, DOM, cores)
    w1, w2, w_back = pl.pallas_call(
        prepare_kernel,
        out_shape=(
            jax.ShapeDtypeStruct((C, TAPS * C), BF16),
            jax.ShapeDtypeStruct((V, TAPS * C), BF16),
            jax.ShapeDtypeStruct((3, C, 3 * VPAD), BF16),
        ),
        in_specs=[VMEM] * 2,
        out_specs=(VMEM,) * 3,
        compiler_params=PARAMS,
    )(w_first, later_kernel_matrix)
    ends = jnp.stack([(dom > 0).astype(F32), (dom < dom_size - 1).astype(F32)])
    obs = jnp.pad(observed_state.reshape(V, CELLS), ((0, FIRST + SHARE - V), (0, 0)))
    area = land.reshape(1, CELLS)
    me = lax.axis_index(ENS).reshape(1)
    stages = (("c", 2), ("x", 4), (Y, 8))
    holder = jnp.bool_(True)
    row, size = LOSS, FLAT
    flags, places = [], []
    for axes, n in stages:
        size //= n
        holder = holder & (lax.axis_index(axes) == row // size)
        row %= size
        flags.append(holder.astype(jnp.int32).reshape(1))
        places.append((row, size))
    across, obs, area, me, ends, flags = lax.optimization_barrier(
        (across, obs, area, me, ends, flags)
    )
    hidden, slope, outlook, sent = pl.pallas_call(
        forward_kernel,
        out_shape=(
            jax.ShapeDtypeStruct((C, 4 * LON), BF16),
            jax.ShapeDtypeStruct((C, 4 * LON), F32),
            jax.ShapeDtypeStruct((V, CELLS), F32),
            jax.ShapeDtypeStruct((MEMBERS, SHARE, LANES), BF16),
        ),
        in_specs=[SMEM] * 2 + [VMEM] * 5,
        out_specs=(VMEM,) * 4,
        scratch_shapes=[pltpu.VMEM((3 * C, 4 * LON), BF16)],
        compiler_params=PARAMS,
    )(core, ends, across, local, beside, w1, w2)

    every = exchange(sent, ENS)
    errors, loss = pl.pallas_call(
        lambda *refs: score_kernel(points, *refs),
        out_shape=(
            jax.ShapeDtypeStruct((MEMBERS, SHARE, LANES), BF16),
            jax.ShapeDtypeStruct((1, 1), F32),
        ),
        in_specs=[SMEM] + [VMEM] * 3,
        out_specs=(VMEM,) * 2,
        compiler_params=PARAMS,
    )(me, every, obs, area)
    errors = exchange(errors, ENS)

    theirs, e, pg, trunk = pl.pallas_call(
        backward_kernel,
        out_shape=(
            jax.ShapeDtypeStruct((HALF, LANES), BF16),
            jax.ShapeDtypeStruct((3 * VPAD, CELLS), BF16),
            jax.ShapeDtypeStruct((3 * C, 4 * LON), BF16),
            jax.ShapeDtypeStruct((C, 6 * LON), BF16),
        ),
        in_specs=[SMEM] + [VMEM] * 8,
        out_specs=(VMEM,) * 4,
        compiler_params=PARAMS,
    )(core, loss, errors, w_back, slope, hidden, across, local, beside)
    mine = pl.pallas_call(
        own_half_kernel,
        out_shape=jax.ShapeDtypeStruct((HALF, LANES), BF16),
        in_specs=[SMEM] + [VMEM] * 5,
        out_specs=VMEM,
        compiler_params=PARAMS,
    )(core, loss, hidden, e, pg, trunk)

    swap = [(0, 1), (1, 0)]
    theirs = lax.ppermute(theirs, "c", swap)
    part = None
    for (axes, n), flag, (row, size) in zip(stages, flags, places):
        if part is None:
            part = summed(row, flag, 1, mine[None], theirs[None])
        else:
            part = exchange(part.reshape(n, size, LANES), axes)
            part = summed(row, flag, 8 if axes == Y else 1, part)
    part = summed(row, flag, 8, exchange(part, "z"))
    part = exchange(part, Y).reshape(8 * size, LANES)
    part = lax.all_gather(part, "x", axis=0, tiled=True)
    other = lax.ppermute(part, "c", swap)
    other, outlook = lax.optimization_barrier((other, outlook.reshape(1, V, ROWS, LON)))
    first, second, loss = pl.pallas_call(
        last_kernel,
        out_shape=(
            jax.ShapeDtypeStruct((C, TAPS * C), BF16),
            jax.ShapeDtypeStruct((V, TAPS * C), BF16),
            jax.ShapeDtypeStruct((1, 1), F32),
        ),
        in_specs=[SMEM, VMEM, VMEM],
        out_specs=(VMEM,) * 3,
        compiler_params=PARAMS,
    )(core, part, other)
    return outlook, first, second, loss.reshape(())


def solution(mesh):
    split_mesh = Mesh(mesh.devices.reshape(tuple(PARTS.values())), tuple(PARTS))
    placed = (P(ENS, None, DOM, None), P(), P(), P(None, DOM, None), P(DOM, None))
    return jax.shard_map(
        body,
        mesh=split_mesh,
        in_specs=placed,
        out_specs=(P(ENS, None, DOM, None), P(), P(), P()),
        check_vma=False,
    )
```

```python
import jax
import jax.numpy as jnp
from jax import lax
from jax.experimental import pallas as pl
from jax.experimental.pallas import tpu as pltpu
from jax.sharding import Mesh
from jax.sharding import PartitionSpec as P

SOFTNESS = 0.25
LAND_WEIGHT = 2.0
LOSS_SCALE = 65536.0
GELU_A = 0.7978845608028654
GELU_B = 0.044715

ENS = ("x", "yh")
DOM = ("zh", "zl", "yl", "c")
Z = ("zl", "zh")
Y = ("yl", "yh")
PARTS = {"x": 4, "yh": 2, "zh": 2, "zl": 4, "yl": 4, "c": 2}
F32 = jnp.float32
BF16 = jnp.bfloat16

C = 256
V = 100
LON = 256
ROWS = 2
CELLS = ROWS * LON
MEMBERS = 8
FIRST = 48
SHARE = 56
VPAD = 112
TAPS = 9
LANES = 128
TILES = TAPS * C // LANES
SECOND = TILES * C
LOSS = SECOND + TILES * VPAD
FLAT = 6656
HALF = FLAT // 2
VMEM = pl.BlockSpec(memory_space=pltpu.VMEM)
SMEM = pl.BlockSpec(memory_space=pltpu.SMEM)
PARAMS = pltpu.CompilerParams(vmem_limit_bytes=40 * 1024 * 1024)
NT = (((1,), (1,)), ((), ()))


def turn(values, shift):
    return values if shift % LON == 0 else pltpu.roll(values, shift % LON, 1)


def dot(a, b):
    return jnp.dot(a, b, preferred_element_type=F32)


def by_side(core, across, beside, use):
    pl.when(core[0] == 0)(lambda: use(across, beside) and None)
    pl.when(core[0] == 1)(lambda: use(beside, across) and None)


def split(total):
    high = total.astype(BF16)
    return high, (total - high.astype(F32)).astype(BF16)


def prepare_kernel(w1, w2, w1_out, w2_out, w_back):
    w1_out[...] = w1[...]
    w2_out[...] = w2[...]
    spare = jnp.zeros((C, VPAD - V), F32)
    for a in range(3):
        turned = []
        for b in range(3):
            tap = w2[:, (3 * a + b) * C : (3 * a + b + 1) * C].astype(F32)
            turned += [tap.T, spare]
        w_back[a] = jnp.concatenate(turned, axis=1).astype(BF16)


def forward_kernel(core, ends, across, local, beside, w1, w2, hidden, slope, outlook, sent, stack):
    wide = ROWS + 2

    def fill(chosen, ref):
        for a in range(3):
            for i in range(wide):
                if (i + a) // 2 == chosen:
                    row = ref[:, (i + a) % 2 * LON : ((i + a) % 2 + 1) * LON]
                    stack[a * C : (a + 1) * C, i * LON : (i + 1) * LON] = row

    fill(1, local)
    by_side(core, across, beside, lambda before, after: (fill(0, before), fill(2, after)))
    for i in range(wide):
        lanes = slice(i * LON, (i + 1) * LON)
        pre = None
        for b in range(3):
            taps = jnp.concatenate(
                [w1[:, (3 * a + b) * C : (3 * a + b + 1) * C] for a in range(3)], axis=1
            )
            part = turn(dot(taps, stack[:, lanes]), 1 - b)
            pre = part if pre is None else pre + part
        square = pre * pre
        t = jnp.tanh(GELU_A * pre * (1.0 + GELU_B * square))
        half = 0.5 * (1.0 + t)
        value = pre * half
        if i == 0:
            value = value * ends[0]
        if i == wide - 1:
            value = value * ends[1]
        hidden[:, lanes] = value.astype(BF16)
        steep = half + (0.5 * GELU_A) * pre * (1.0 - t * t) * (1.0 + 3.0 * GELU_B * square)
        if i == 0:
            steep = steep * ends[0]
        if i == wide - 1:
            steep = steep * ends[1]
        slope[:, lanes] = steep
    spare = jnp.zeros((FIRST + SHARE - V, LON), F32)
    for i in range(ROWS):
        total = None
        for b in range(3):
            part = None
            for a in range(3):
                tap = w2[:, (3 * a + b) * C : (3 * a + b + 1) * C]
                term = dot(tap, hidden[:, (i + a) * LON : (i + a + 1) * LON])
                part = term if part is None else part + term
            part = turn(part, 1 - b)
            total = part if total is None else total + part
        lanes = slice(i * LON, (i + 1) * LON)
        outlook[:, lanes] = total
        padded = jnp.concatenate([total, spare], axis=0)
        for part in range(2):
            tile = padded[:, part * LANES : (part + 1) * LANES]
            sent[2 * i + part] = tile[:SHARE].astype(BF16)
            sent[4 + 2 * i + part] = tile[FIRST:].astype(BF16)


def score_kernel(points, me, every, obs, land, errors, loss):
    half = me[0] // 4
    cells = pl.ds(pl.multiple_of(me[0] % 4 * LANES, LANES), LANES)
    area = 1.0 + LAND_WEIGHT * land[:, cells].astype(F32)
    x = [every[p].astype(F32) for p in range(MEMBERS)]
    truth = obs[pl.ds(pl.multiple_of(half * FIRST, FIRST), SHARE), cells]
    count = MEMBERS * (MEMBERS - 1)
    skill = pairs = jnp.zeros((SHARE, LANES), F32)
    slopes = []
    for p in range(MEMBERS):
        d = x[p] - truth
        square = d * d + SOFTNESS * SOFTNESS
        inverse = lax.rsqrt(square)
        skill = skill + square * inverse
        slopes.append(d * inverse * (1.0 / MEMBERS))
    for p in range(MEMBERS):
        for q in range(p + 1, MEMBERS):
            d = x[p] - x[q]
            square = d * d + SOFTNESS * SOFTNESS
            inverse = lax.rsqrt(square)
            pairs = pairs + square * inverse
            s = d * inverse * (1.0 / count)
            slopes[p] = slopes[p] - s
            slopes[q] = slopes[q] + s
    variable = lax.broadcasted_iota(jnp.int32, (SHARE, LANES), 0)
    crps = area * (skill * (1.0 / MEMBERS) - pairs * (1.0 / count))
    crps = jnp.where(variable < jnp.where(half == 0, FIRST, V - FIRST), crps, 0.0)
    loss[...] = jnp.sum(crps, axis=(0, 1), keepdims=True) * (1.0 / points)
    factor = area * (LOSS_SCALE / points)
    for p in range(MEMBERS):
        errors[p] = (factor * slopes[p]).astype(BF16)


def backward_kernel(
    core, loss, err, w_back, slope, hidden, across, local, beside, theirs, e, pg, trunk
):
    trunk[:, 2 * LON : 4 * LON] = local[...]

    def fill(before, after):
        trunk[:, : 2 * LON] = before[...]
        trunk[:, 4 * LON :] = after[...]

    by_side(core, across, beside, fill)
    for i in range(ROWS):
        spare = jnp.zeros((VPAD - FIRST - SHARE, LANES), F32)
        tiles = []
        for tile in (2 * i, 2 * i + 1):
            lower, upper = err[tile].astype(F32)[:FIRST], err[4 + tile].astype(F32)
            tiles.append(jnp.concatenate([lower, upper, spare], axis=0))
        row = jnp.concatenate(tiles, axis=1)
        for b in range(3):
            e[b * VPAD : (b + 1) * VPAD, i * LON : (i + 1) * LON] = turn(row, b - 1).astype(BF16)
    wide = ROWS + 2
    for i in range(wide):
        back = None
        for a in range(3):
            if 0 <= i - a < ROWS:
                term = dot(w_back[a], e[:, (i - a) * LON : (i - a + 1) * LON])
                back = term if back is None else back + term
        lanes = slice(i * LON, (i + 1) * LON)
        grad = back * slope[:, lanes]
        for b in range(3):
            pg[b * C : (b + 1) * C, lanes] = turn(grad, b - 1).astype(BF16)
    pl.when(core[0] == 0)(lambda: lower_half(loss, hidden, e, pg, trunk, theirs))
    pl.when(core[0] == 1)(lambda: upper_half(pg, trunk, theirs))


def own_half_kernel(core, loss, hidden, e, pg, trunk, mine):
    pl.when(core[0] == 0)(lambda: upper_half(pg, trunk, mine))
    pl.when(core[0] == 1)(lambda: lower_half(loss, hidden, e, pg, trunk, mine))


def first_tiles(pg, trunk, tiles, out, start):
    a = tiles[0] // 6
    window = trunk[:, a * LON : (a + ROWS + 2) * LON]
    head, tail = tiles[0] % 6 // 2, tiles[-1] % 6 // 2
    both = lax.dot_general(
        pg[head * C : (tail + 1) * C, :], window, NT, preferred_element_type=F32
    )
    for tile in tiles:
        b, part = tile % 6 // 2 - head, tile % 2
        value = both[b * C : (b + 1) * C, part * LANES : (part + 1) * LANES]
        out[tile * C - start : (tile + 1) * C - start, :] = value.astype(BF16)


def upper_half(pg, trunk, out):
    for tiles in (range(6), range(6, 12), range(12, 13)):
        first_tiles(pg, trunk, tiles, out, 0)


def lower_half(loss, hidden, e, pg, trunk, out):
    first_tiles(pg, trunk, range(13, 18), out, HALF)
    for a in range(3):
        reach = hidden[:, a * LON : a * LON + CELLS]
        seconds = lax.dot_general(e[...], reach, NT, preferred_element_type=F32)
        for b in range(3):
            second = seconds[b * VPAD : (b + 1) * VPAD].astype(BF16)
            for part in range(2):
                at = SECOND + (2 * (3 * a + b) + part) * VPAD - HALF
                out[at : at + VPAD, :] = second[:, part * LANES : (part + 1) * LANES]
    high, low = split(jnp.broadcast_to(loss[...], (1, LANES)))
    index = lax.broadcasted_iota(jnp.int32, (16, LANES), 0)
    both = jnp.where(index == 0, high.astype(F32), jnp.where(index == 1, low.astype(F32), 0.0))
    at = LOSS - HALF
    out[at : at + 16, :] = both.astype(BF16)
    out[at + 16 :, :] = jnp.zeros((HALF - at - 16, LANES), BF16)


def sum_kernel(row, holder, *refs):
    out = refs[-1]

    def total(at, n):
        value = None
        for parts in refs[:-1]:
            for i in range(parts.shape[0]):
                term = parts[i, at : at + n].astype(F32)
                value = term if value is None else value + term
        return value

    copies, size = out.shape[:2]
    value = total(0, size).astype(BF16)
    for i in range(copies):
        out[i] = value
    base, span = (row, 16) if row % 16 == 0 else (0, size)

    @pl.when(holder[0] == 1)
    def _():
        here = total(base, span)
        high, low = split(here[row - base : row - base + 1] + here[row - base + 1 : row - base + 2])
        index = lax.broadcasted_iota(jnp.int32, (span, LANES), 0) + base
        fixed = jnp.where(index == row, high.astype(F32), here)
        fixed = jnp.where(index == row + 1, low.astype(F32), fixed)
        for i in range(copies):
            out[i, base : base + span, :] = fixed.astype(BF16)


def summed(row, holder, copies, *arrays):
    body = lambda *refs: sum_kernel(row, *refs)
    return pl.pallas_call(
        body,
        out_shape=jax.ShapeDtypeStruct((copies,) + arrays[0].shape[1:], BF16),
        in_specs=[SMEM] + [VMEM] * len(arrays),
        out_specs=VMEM,
        compiler_params=PARAMS,
    )(holder, *arrays)


def last_kernel(core, own, other, first, second, loss):
    def assemble(low, high):
        def flat(at, n):
            return low[at : at + n, :] if at < HALF else high[at - HALF : at - HALF + n, :]

        for tile in range(TILES):
            lanes = slice(tile * LANES, (tile + 1) * LANES)
            first[:, lanes] = flat(tile * C, C)
            second[:, lanes] = flat(SECOND + tile * VPAD, VPAD)[:V]
        here = flat(LOSS, 16).astype(F32)
        loss[...] = here[0:1, 0:1] + here[1:2, 0:1]

    pl.when(core[0] == 0)(lambda: assemble(own, other))
    pl.when(core[0] == 1)(lambda: assemble(other, own))


def exchange(array, axes):
    return lax.all_to_all(array, axes, 0, 0, tiled=True)


def body(features, w_first, later_kernel_matrix, observed_state, land):
    dom_size = lax.axis_size(DOM)
    dom = lax.axis_index(DOM)
    chips = [(i, i + 1) for i in range(1, dom_size - 1, 2)]
    chips += [(j, i) for i, j in chips]
    cores = [(i, i ^ 1) for i in range(dom_size)]
    side = lax.axis_index("c")
    core = side.reshape(1)
    points = float(V * ROWS * dom_size * LON)

    local = features.reshape(C, CELLS)
    across = lax.ppermute(local, DOM, chips)
    beside = lax.ppermute(local, DOM, cores)
    w1, w2, w_back = pl.pallas_call(
        prepare_kernel,
        out_shape=(
            jax.ShapeDtypeStruct((C, TAPS * C), BF16),
            jax.ShapeDtypeStruct((V, TAPS * C), BF16),
            jax.ShapeDtypeStruct((3, C, 3 * VPAD), BF16),
        ),
        in_specs=[VMEM] * 2,
        out_specs=(VMEM,) * 3,
        compiler_params=PARAMS,
    )(w_first, later_kernel_matrix)
    ends = jnp.stack([(dom > 0).astype(F32), (dom < dom_size - 1).astype(F32)])
    obs = jnp.pad(observed_state.reshape(V, CELLS), ((0, FIRST + SHARE - V), (0, 0)))
    area = land.reshape(1, CELLS)
    me = lax.axis_index(("yh", "x")).reshape(1)
    stages = (("c", 2), ("x", 4), (Y, 8))
    holder = jnp.bool_(True)
    row, size = LOSS, FLAT
    flags, places = [], []
    for axes, n in stages:
        size //= n
        holder = holder & (lax.axis_index(axes) == row // size)
        row %= size
        flags.append(holder.astype(jnp.int32).reshape(1))
        places.append((row, size))
    across, obs, area, me, ends, flags = lax.optimization_barrier(
        (across, obs, area, me, ends, flags)
    )
    hidden, slope, outlook, sent = pl.pallas_call(
        forward_kernel,
        out_shape=(
            jax.ShapeDtypeStruct((C, 4 * LON), BF16),
            jax.ShapeDtypeStruct((C, 4 * LON), F32),
            jax.ShapeDtypeStruct((V, CELLS), F32),
            jax.ShapeDtypeStruct((MEMBERS, SHARE, LANES), BF16),
        ),
        in_specs=[SMEM] * 2 + [VMEM] * 5,
        out_specs=(VMEM,) * 4,
        scratch_shapes=[pltpu.VMEM((3 * C, 4 * LON), BF16)],
        compiler_params=PARAMS,
    )(core, ends, across, local, beside, w1, w2)

    every = exchange(sent, ("yh", "x"))
    errors, loss = pl.pallas_call(
        lambda *refs: score_kernel(points, *refs),
        out_shape=(
            jax.ShapeDtypeStruct((MEMBERS, SHARE, LANES), BF16),
            jax.ShapeDtypeStruct((1, 1), F32),
        ),
        in_specs=[SMEM] + [VMEM] * 3,
        out_specs=(VMEM,) * 2,
        compiler_params=PARAMS,
    )(me, every, obs, area)
    errors = exchange(errors, ("yh", "x"))

    theirs, e, pg, trunk = pl.pallas_call(
        backward_kernel,
        out_shape=(
            jax.ShapeDtypeStruct((HALF, LANES), BF16),
            jax.ShapeDtypeStruct((3 * VPAD, CELLS), BF16),
            jax.ShapeDtypeStruct((3 * C, 4 * LON), BF16),
            jax.ShapeDtypeStruct((C, 6 * LON), BF16),
        ),
        in_specs=[SMEM] + [VMEM] * 8,
        out_specs=(VMEM,) * 4,
        compiler_params=PARAMS,
    )(core, loss, errors, w_back, slope, hidden, across, local, beside)
    mine = pl.pallas_call(
        own_half_kernel,
        out_shape=jax.ShapeDtypeStruct((HALF, LANES), BF16),
        in_specs=[SMEM] + [VMEM] * 5,
        out_specs=VMEM,
        compiler_params=PARAMS,
    )(core, loss, hidden, e, pg, trunk)

    swap = [(0, 1), (1, 0)]
    theirs = lax.ppermute(theirs, "c", swap)
    part = None
    for (axes, n), flag, (row, size) in zip(stages, flags, places):
        if part is None:
            part = summed(row, flag, 1, mine[None], theirs[None])
        else:
            part = exchange(part.reshape(n, size, LANES), axes)
            part = summed(row, flag, 8 if axes == Y else 1, part)
    part = summed(row, flag, 8, exchange(part, Z))
    part = exchange(part, Y).reshape(8 * size, LANES)
    part = lax.all_gather(part, "x", axis=0, tiled=True)
    other = lax.ppermute(part, "c", swap)
    other, outlook = lax.optimization_barrier((other, outlook.reshape(1, V, ROWS, LON)))
    first, second, loss = pl.pallas_call(
        last_kernel,
        out_shape=(
            jax.ShapeDtypeStruct((C, TAPS * C), BF16),
            jax.ShapeDtypeStruct((V, TAPS * C), BF16),
            jax.ShapeDtypeStruct((1, 1), F32),
        ),
        in_specs=[SMEM, VMEM, VMEM],
        out_specs=(VMEM,) * 3,
        compiler_params=PARAMS,
    )(core, part, other)
    return outlook, first, second, loss.reshape(())


def solution(mesh):
    split_mesh = Mesh(mesh.devices.reshape(tuple(PARTS.values())), tuple(PARTS))
    placed = (P(ENS, None, DOM, None), P(), P(), P(None, DOM, None), P(DOM, None))
    return jax.shard_map(
        body,
        mesh=split_mesh,
        in_specs=placed,
        out_specs=(P(ENS, None, DOM, None), P(), P(), P()),
        check_vma=False,
    )
```

```python
import jax
import jax.numpy as jnp
from jax import lax
from jax.experimental import pallas as pl
from jax.experimental.pallas import tpu as pltpu
from jax.sharding import Mesh
from jax.sharding import PartitionSpec as P

SOFTNESS = 0.25
LAND_WEIGHT = 2.0
LOSS_SCALE = 65536.0
GELU_A = 0.7978845608028654
GELU_B = 0.044715

ENS = ("x", "yh")
DOM = ("zh", "zl", "yl", "c")
Z = ("zl", "zh")
Y = ("yl", "yh")
PARTS = {"x": 4, "yh": 2, "zh": 2, "zl": 4, "yl": 4, "c": 2}
F32 = jnp.float32
BF16 = jnp.bfloat16

C = 256
V = 100
LON = 256
ROWS = 2
CELLS = ROWS * LON
MEMBERS = 8
FIRST = 48
SHARE = 56
VPAD = 112
TAPS = 9
LANES = 128
TILES = TAPS * C // LANES
SECOND = TILES * C
LOSS = SECOND + TILES * VPAD
FLAT = 6656
HALF = FLAT // 2
VMEM = pl.BlockSpec(memory_space=pltpu.VMEM)
SMEM = pl.BlockSpec(memory_space=pltpu.SMEM)
PARAMS = pltpu.CompilerParams(vmem_limit_bytes=40 * 1024 * 1024)
NT = (((1,), (1,)), ((), ()))


def turn(values, shift):
    return values if shift % LON == 0 else pltpu.roll(values, shift % LON, 1)


def dot(a, b):
    return jnp.dot(a, b, preferred_element_type=F32)


def by_side(core, across, beside, use):
    pl.when(core[0] == 0)(lambda: use(across, beside) and None)
    pl.when(core[0] == 1)(lambda: use(beside, across) and None)


def split(total):
    high = total.astype(BF16)
    return high, (total - high.astype(F32)).astype(BF16)


def prepare_kernel(w1, w2, w1_out, w2_out, w_back):
    w1_out[...] = w1[...]
    w2_out[...] = w2[...]
    spare = jnp.zeros((C, VPAD - V), F32)
    for a in range(3):
        turned = []
        for b in range(3):
            tap = w2[:, (3 * a + b) * C : (3 * a + b + 1) * C].astype(F32)
            turned += [tap.T, spare]
        w_back[a] = jnp.concatenate(turned, axis=1).astype(BF16)


def taps_of(w1, b, a, n):
    return jnp.concatenate(
        [w1[:, (3 * k + b) * C : (3 * k + b + 1) * C] for k in range(a, a + n)], axis=1
    )


def own_kernel(local, w1, partial, stack):
    upper, lower = local[:, :LON], local[:, LON:]
    stack[:C, :] = upper
    stack[C:, :] = lower
    for i in range(ROWS + 2):
        a = max(ROWS - i, 0)
        rows = (upper, stack, stack, lower)[i]
        total = None
        for b in range(3):
            part = turn(dot(taps_of(w1, b, a, (1, 2, 2, 1)[i]), rows[...]), 1 - b)
            total = part if total is None else total + part
        partial[:, i * LON : (i + 1) * LON] = total


def forward_kernel(
    core, ends, partial, across, beside, w1, w2, hidden, slope, outlook, sent, stack
):
    wide = ROWS + 2

    def fill(before, after):
        stack[:C, :LON] = before[:, :LON]
        stack[C:, :LON] = before[:, LON:]
        stack[:C, LON:] = after[:, :LON]
        stack[C:, LON:] = after[:, LON:]

    by_side(core, across, beside, fill)
    for i in range(wide):
        lanes = slice(i * LON, (i + 1) * LON)
        side = slice(0, LON) if i < 2 else slice(LON, 2 * LON)
        at = (slice(0, 2 * C), slice(C, 2 * C), slice(0, C), slice(0, 2 * C))[i]
        a, n = ((0, 2), (0, 1), (2, 1), (1, 2))[i]
        pre = partial[:, lanes]
        for b in range(3):
            pre = pre + turn(dot(taps_of(w1, b, a, n), stack[at, side]), 1 - b)
        square = pre * pre
        t = jnp.tanh(GELU_A * pre * (1.0 + GELU_B * square))
        half = 0.5 * (1.0 + t)
        value = pre * half
        if i == 0:
            value = value * ends[0]
        if i == wide - 1:
            value = value * ends[1]
        hidden[:, lanes] = value.astype(BF16)
        steep = half + (0.5 * GELU_A) * pre * (1.0 - t * t) * (1.0 + 3.0 * GELU_B * square)
        if i == 0:
            steep = steep * ends[0]
        if i == wide - 1:
            steep = steep * ends[1]
        slope[:, lanes] = steep
    spare = jnp.zeros((FIRST + SHARE - V, LON), F32)
    for i in range(ROWS):
        total = None
        for b in range(3):
            part = None
            for a in range(3):
                tap = w2[:, (3 * a + b) * C : (3 * a + b + 1) * C]
                term = dot(tap, hidden[:, (i + a) * LON : (i + a + 1) * LON])
                part = term if part is None else part + term
            part = turn(part, 1 - b)
            total = part if total is None else total + part
        lanes = slice(i * LON, (i + 1) * LON)
        outlook[:, lanes] = total
        padded = jnp.concatenate([total, spare], axis=0)
        for part in range(2):
            tile = padded[:, part * LANES : (part + 1) * LANES]
            sent[2 * i + part] = tile[:SHARE].astype(BF16)
            sent[4 + 2 * i + part] = tile[FIRST:].astype(BF16)


def score_kernel(points, me, every, obs, land, errors, loss):
    half = me[0] // 4
    cells = pl.ds(pl.multiple_of(me[0] % 4 * LANES, LANES), LANES)
    area = 1.0 + LAND_WEIGHT * land[:, cells].astype(F32)
    x = [every[p].astype(F32) for p in range(MEMBERS)]
    truth = obs[pl.ds(pl.multiple_of(half * FIRST, FIRST), SHARE), cells]
    count = MEMBERS * (MEMBERS - 1)
    skill = pairs = jnp.zeros((SHARE, LANES), F32)
    slopes = []
    for p in range(MEMBERS):
        d = x[p] - truth
        square = d * d + SOFTNESS * SOFTNESS
        inverse = lax.rsqrt(square)
        skill = skill + square * inverse
        slopes.append(d * inverse * (1.0 / MEMBERS))
    for p in range(MEMBERS):
        for q in range(p + 1, MEMBERS):
            d = x[p] - x[q]
            square = d * d + SOFTNESS * SOFTNESS
            inverse = lax.rsqrt(square)
            pairs = pairs + square * inverse
            s = d * inverse * (1.0 / count)
            slopes[p] = slopes[p] - s
            slopes[q] = slopes[q] + s
    variable = lax.broadcasted_iota(jnp.int32, (SHARE, LANES), 0)
    crps = area * (skill * (1.0 / MEMBERS) - pairs * (1.0 / count))
    crps = jnp.where(variable < jnp.where(half == 0, FIRST, V - FIRST), crps, 0.0)
    loss[...] = jnp.sum(crps, axis=(0, 1), keepdims=True) * (1.0 / points)
    factor = area * (LOSS_SCALE / points)
    for p in range(MEMBERS):
        errors[p] = (factor * slopes[p]).astype(BF16)


def backward_kernel(
    core, loss, err, w_back, slope, hidden, across, local, beside, theirs, e, pg, trunk
):
    trunk[:, 2 * LON : 4 * LON] = local[...]

    def fill(before, after):
        trunk[:, : 2 * LON] = before[...]
        trunk[:, 4 * LON :] = after[...]

    by_side(core, across, beside, fill)
    for i in range(ROWS):
        spare = jnp.zeros((VPAD - FIRST - SHARE, LANES), F32)
        tiles = []
        for tile in (2 * i, 2 * i + 1):
            lower, upper = err[tile].astype(F32)[:FIRST], err[4 + tile].astype(F32)
            tiles.append(jnp.concatenate([lower, upper, spare], axis=0))
        row = jnp.concatenate(tiles, axis=1)
        for b in range(3):
            e[b * VPAD : (b + 1) * VPAD, i * LON : (i + 1) * LON] = turn(row, b - 1).astype(BF16)
    wide = ROWS + 2
    for i in range(wide):
        back = None
        for a in range(3):
            if 0 <= i - a < ROWS:
                term = dot(w_back[a], e[:, (i - a) * LON : (i - a + 1) * LON])
                back = term if back is None else back + term
        lanes = slice(i * LON, (i + 1) * LON)
        grad = back * slope[:, lanes]
        for b in range(3):
            pg[b * C : (b + 1) * C, lanes] = turn(grad, b - 1).astype(BF16)
    pl.when(core[0] == 0)(lambda: lower_half(loss, hidden, e, pg, trunk, theirs))
    pl.when(core[0] == 1)(lambda: upper_half(pg, trunk, theirs))


def own_half_kernel(core, loss, hidden, e, pg, trunk, mine):
    pl.when(core[0] == 0)(lambda: upper_half(pg, trunk, mine))
    pl.when(core[0] == 1)(lambda: lower_half(loss, hidden, e, pg, trunk, mine))


def first_tiles(pg, trunk, tiles, out, start):
    a = tiles[0] // 6
    window = trunk[:, a * LON : (a + ROWS + 2) * LON]
    head, tail = tiles[0] % 6 // 2, tiles[-1] % 6 // 2
    both = lax.dot_general(
        pg[head * C : (tail + 1) * C, :], window, NT, preferred_element_type=F32
    )
    for tile in tiles:
        b, part = tile % 6 // 2 - head, tile % 2
        value = both[b * C : (b + 1) * C, part * LANES : (part + 1) * LANES]
        out[tile * C - start : (tile + 1) * C - start, :] = value.astype(BF16)


def upper_half(pg, trunk, out):
    for tiles in (range(6), range(6, 12), range(12, 13)):
        first_tiles(pg, trunk, tiles, out, 0)


def lower_half(loss, hidden, e, pg, trunk, out):
    first_tiles(pg, trunk, range(13, 18), out, HALF)
    for a in range(3):
        reach = hidden[:, a * LON : a * LON + CELLS]
        seconds = lax.dot_general(e[...], reach, NT, preferred_element_type=F32)
        for b in range(3):
            second = seconds[b * VPAD : (b + 1) * VPAD].astype(BF16)
            for part in range(2):
                at = SECOND + (2 * (3 * a + b) + part) * VPAD - HALF
                out[at : at + VPAD, :] = second[:, part * LANES : (part + 1) * LANES]
    high, low = split(jnp.broadcast_to(loss[...], (1, LANES)))
    index = lax.broadcasted_iota(jnp.int32, (16, LANES), 0)
    both = jnp.where(index == 0, high.astype(F32), jnp.where(index == 1, low.astype(F32), 0.0))
    at = LOSS - HALF
    out[at : at + 16, :] = both.astype(BF16)
    out[at + 16 :, :] = jnp.zeros((HALF - at - 16, LANES), BF16)


def sum_kernel(row, holder, *refs):
    out = refs[-1]

    def total(at, n):
        value = None
        for parts in refs[:-1]:
            for i in range(parts.shape[0]):
                term = parts[i, at : at + n].astype(F32)
                value = term if value is None else value + term
        return value

    copies, size = out.shape[:2]
    value = total(0, size).astype(BF16)
    for i in range(copies):
        out[i] = value
    base, span = (row, 16) if row % 16 == 0 else (0, size)

    @pl.when(holder[0] == 1)
    def _():
        here = total(base, span)
        high, low = split(here[row - base : row - base + 1] + here[row - base + 1 : row - base + 2])
        index = lax.broadcasted_iota(jnp.int32, (span, LANES), 0) + base
        fixed = jnp.where(index == row, high.astype(F32), here)
        fixed = jnp.where(index == row + 1, low.astype(F32), fixed)
        for i in range(copies):
            out[i, base : base + span, :] = fixed.astype(BF16)


def summed(row, holder, copies, *arrays):
    body = lambda *refs: sum_kernel(row, *refs)
    return pl.pallas_call(
        body,
        out_shape=jax.ShapeDtypeStruct((copies,) + arrays[0].shape[1:], BF16),
        in_specs=[SMEM] + [VMEM] * len(arrays),
        out_specs=VMEM,
        compiler_params=PARAMS,
    )(holder, *arrays)


def last_kernel(core, own, other, first, second, loss):
    def assemble(low, high):
        def flat(at, n):
            return low[at : at + n, :] if at < HALF else high[at - HALF : at - HALF + n, :]

        for tile in range(TILES):
            lanes = slice(tile * LANES, (tile + 1) * LANES)
            first[:, lanes] = flat(tile * C, C)
            second[:, lanes] = flat(SECOND + tile * VPAD, VPAD)[:V]
        here = flat(LOSS, 16).astype(F32)
        loss[...] = here[0:1, 0:1] + here[1:2, 0:1]

    pl.when(core[0] == 0)(lambda: assemble(own, other))
    pl.when(core[0] == 1)(lambda: assemble(other, own))


def exchange(array, axes):
    return lax.all_to_all(array, axes, 0, 0, tiled=True)


def body(features, w_first, later_kernel_matrix, observed_state, land):
    dom_size = lax.axis_size(DOM)
    dom = lax.axis_index(DOM)
    chips = [(i, i + 1) for i in range(1, dom_size - 1, 2)]
    chips += [(j, i) for i, j in chips]
    cores = [(i, i ^ 1) for i in range(dom_size)]
    side = lax.axis_index("c")
    core = side.reshape(1)
    points = float(V * ROWS * dom_size * LON)

    local = features.reshape(C, CELLS)
    across = lax.ppermute(local, DOM, chips)
    beside = lax.ppermute(local, DOM, cores)
    w1, w2, w_back = pl.pallas_call(
        prepare_kernel,
        out_shape=(
            jax.ShapeDtypeStruct((C, TAPS * C), BF16),
            jax.ShapeDtypeStruct((V, TAPS * C), BF16),
            jax.ShapeDtypeStruct((3, C, 3 * VPAD), BF16),
        ),
        in_specs=[VMEM] * 2,
        out_specs=(VMEM,) * 3,
        compiler_params=PARAMS,
    )(w_first, later_kernel_matrix)
    partial = pl.pallas_call(
        own_kernel,
        out_shape=jax.ShapeDtypeStruct((C, 4 * LON), F32),
        in_specs=[VMEM] * 2,
        out_specs=VMEM,
        scratch_shapes=[pltpu.VMEM((2 * C, LON), BF16)],
        compiler_params=PARAMS,
    )(local, w1)
    ends = jnp.stack([(dom > 0).astype(F32), (dom < dom_size - 1).astype(F32)])
    obs = jnp.pad(observed_state.reshape(V, CELLS), ((0, FIRST + SHARE - V), (0, 0)))
    area = land.reshape(1, CELLS)
    me = lax.axis_index(("yh", "x")).reshape(1)
    stages = (("c", 2), ("x", 4), (Y, 8))
    holder = jnp.bool_(True)
    row, size = LOSS, FLAT
    flags, places = [], []
    for axes, n in stages:
        size //= n
        holder = holder & (lax.axis_index(axes) == row // size)
        row %= size
        flags.append(holder.astype(jnp.int32).reshape(1))
        places.append((row, size))
    across, obs, area, me, ends, flags, partial = lax.optimization_barrier(
        (across, obs, area, me, ends, flags, partial)
    )
    hidden, slope, outlook, sent = pl.pallas_call(
        forward_kernel,
        out_shape=(
            jax.ShapeDtypeStruct((C, 4 * LON), BF16),
            jax.ShapeDtypeStruct((C, 4 * LON), F32),
            jax.ShapeDtypeStruct((V, CELLS), F32),
            jax.ShapeDtypeStruct((MEMBERS, SHARE, LANES), BF16),
        ),
        in_specs=[SMEM] * 2 + [VMEM] * 5,
        out_specs=(VMEM,) * 4,
        scratch_shapes=[pltpu.VMEM((2 * C, 2 * LON), BF16)],
        compiler_params=PARAMS,
    )(core, ends, partial, across, beside, w1, w2)

    every = exchange(sent, ("yh", "x"))
    errors, loss = pl.pallas_call(
        lambda *refs: score_kernel(points, *refs),
        out_shape=(
            jax.ShapeDtypeStruct((MEMBERS, SHARE, LANES), BF16),
            jax.ShapeDtypeStruct((1, 1), F32),
        ),
        in_specs=[SMEM] + [VMEM] * 3,
        out_specs=(VMEM,) * 2,
        compiler_params=PARAMS,
    )(me, every, obs, area)
    errors = exchange(errors, ("yh", "x"))

    theirs, e, pg, trunk = pl.pallas_call(
        backward_kernel,
        out_shape=(
            jax.ShapeDtypeStruct((HALF, LANES), BF16),
            jax.ShapeDtypeStruct((3 * VPAD, CELLS), BF16),
            jax.ShapeDtypeStruct((3 * C, 4 * LON), BF16),
            jax.ShapeDtypeStruct((C, 6 * LON), BF16),
        ),
        in_specs=[SMEM] + [VMEM] * 8,
        out_specs=(VMEM,) * 4,
        compiler_params=PARAMS,
    )(core, loss, errors, w_back, slope, hidden, across, local, beside)
    mine = pl.pallas_call(
        own_half_kernel,
        out_shape=jax.ShapeDtypeStruct((HALF, LANES), BF16),
        in_specs=[SMEM] + [VMEM] * 5,
        out_specs=VMEM,
        compiler_params=PARAMS,
    )(core, loss, hidden, e, pg, trunk)

    swap = [(0, 1), (1, 0)]
    theirs = lax.ppermute(theirs, "c", swap)
    part = None
    for (axes, n), flag, (row, size) in zip(stages, flags, places):
        if part is None:
            part = summed(row, flag, 1, mine[None], theirs[None])
        else:
            part = exchange(part.reshape(n, size, LANES), axes)
            part = summed(row, flag, 8 if axes == Y else 1, part)
    part = summed(row, flag, 8, exchange(part, Z))
    part = exchange(part, Y).reshape(8 * size, LANES)
    part = lax.all_gather(part, "x", axis=0, tiled=True)
    other = lax.ppermute(part, "c", swap)
    other, outlook = lax.optimization_barrier((other, outlook.reshape(1, V, ROWS, LON)))
    first, second, loss = pl.pallas_call(
        last_kernel,
        out_shape=(
            jax.ShapeDtypeStruct((C, TAPS * C), BF16),
            jax.ShapeDtypeStruct((V, TAPS * C), BF16),
            jax.ShapeDtypeStruct((1, 1), F32),
        ),
        in_specs=[SMEM, VMEM, VMEM],
        out_specs=(VMEM,) * 3,
        compiler_params=PARAMS,
    )(core, part, other)
    return outlook, first, second, loss.reshape(())


def solution(mesh):
    split_mesh = Mesh(mesh.devices.reshape(tuple(PARTS.values())), tuple(PARTS))
    placed = (P(ENS, None, DOM, None), P(), P(), P(None, DOM, None), P(DOM, None))
    return jax.shard_map(
        body,
        mesh=split_mesh,
        in_specs=placed,
        out_specs=(P(ENS, None, DOM, None), P(), P(), P()),
        check_vma=False,
    )
```
